512 devices in a mesh: seq: 128 (over y, z, core), ch: 4 (over x).
Axes of the slice: x: 4, y: 8, z: 8, core: 2. Of those that a mesh axis runs over, the one named last changes fastest.
Arguments:
- features: bfloat16 [3, 32768, 4096], P(None, 'seq', 'ch'), may hold values from -6 to 6
- short_filter: bfloat16 [3, 7, 4096], P(None, None, 'ch'), may hold values from -2 to 2
- long_filter: bfloat16 [256, 128], replicated, may hold values from -0.5 to 0.5
- grad_out: bfloat16 [32768, 4096], P('seq', 'ch'), may hold values from -6 to 6
Outputs:
- grad_features: bfloat16 [3, 32768, 4096], P(None, 'seq', 'ch')
- grad_short: float32 [3, 7, 4096], P(None, None, 'ch')
- grad_long: float32 [256, 128], replicated
The draws below stay inside these ranges and needn't reach their ends.
All inputs are finite; a program needn't handle non-finite values.
Results may differ from the reference program's by a relative error of at most 0.0073.
Values may be sent and summed in bfloat16 or wider, within the bound.
A program may use at most 64 MiB of HBM per device.

```python
import math
import jax
import jax.numpy as jnp
from jax import lax

D = 4096
GROUP = 16
L_MR = 128
L_SE = 7
GROUPS = 256
TOKENS = 32768


def level_of(key, dims, pieces, least, high):
    factor_of = 1.0
    for position, parts in pieces:
        draws = jax.random.uniform(jax.random.fold_in(jax.random.fold_in(key, 6), position), (parts,), jnp.float32, least / len(pieces), high / len(pieces))
        factor_of = factor_of * jnp.repeat(jnp.exp(draws), dims[position] // parts).reshape((-1,) + (1,) * (len(dims) - 1 - position))
    return factor_of


def normal_values(key, shape, width, bound, pieces=(), kind=jnp.bfloat16):
    array = width * jax.random.normal(key, shape, jnp.float32)
    if pieces:
        array = array * level_of(key, shape, pieces, -0.22, 0.18)
    return jnp.clip(array, -bound, bound).astype(kind)


def setup_inputs(seed: int = 0) -> dict:
    arg_keys = jax.random.split(jax.random.key(seed), 5)
    features = normal_values(arg_keys[0], (3, TOKENS, D), 1.0, 6.0, ((1, 128), (2, 4)))
    short_filter = normal_values(arg_keys[1], (3, L_SE, D), L_SE ** -0.5, 2.0, ((2, 4),))
    long_filter = normal_values(arg_keys[2], (GROUPS, L_MR), L_MR ** -0.5, 0.5)
    grad_out = normal_values(arg_keys[3], (TOKENS, D), 1.0, 6.0, ((0, 128), (1, 4)))
    return dict(features=features, short_filter=short_filter, long_filter=long_filter, grad_out=grad_out)


def causal_sum(signal, taps):
    length = signal.shape[0]
    count = taps.shape[0]
    padded = jnp.pad(signal, ((count - 1, 0), (0, 0)))

    def add_tap(j, total):
        piece = lax.dynamic_slice_in_dim(padded, count - 1 - j, length, 0)
        return total + taps[j].astype(jnp.float32) * piece.astype(jnp.float32)
    return lax.fori_loop(0, count, add_tap, jnp.zeros(signal.shape, jnp.float32))

def later_sum(signal, taps):
    length = signal.shape[0]
    count = taps.shape[0]
    padded = jnp.pad(signal, ((0, count - 1), (0, 0)))

    def add_tap(j, total):
        piece = lax.dynamic_slice_in_dim(padded, j, length, 0)
        return total + taps[j].astype(jnp.float32) * piece.astype(jnp.float32)
    return lax.fori_loop(0, count, add_tap, jnp.zeros(signal.shape, jnp.float32))

def lag_products(cotangent, signal, count):
    length = signal.shape[0]
    padded = jnp.pad(signal, ((count - 1, 0), (0, 0)))
    grad_part = cotangent.astype(jnp.float32)

    def one_lag(j):
        piece = lax.dynamic_slice_in_dim(padded, count - 1 - j, length, 0)
        return lax.optimization_barrier(jnp.sum(grad_part * piece.astype(jnp.float32), axis=0))
    return lax.map(one_lag, jnp.arange(count, dtype=jnp.int32))

def reference(features, short_filter, long_filter, grad_out):
    featured = jnp.stack([causal_sum(features[i], short_filter[i]).astype(jnp.bfloat16) for i in range(3)])
    query_feat, key_feat, value_feat = (featured[0], featured[1], featured[2])
    product = (key_feat.astype(jnp.float32) * value_feat.astype(jnp.float32)).astype(jnp.bfloat16)
    long_taps = jnp.tile(long_filter.T, (1, D // GROUPS))
    filtered = causal_sum(product, long_taps)
    grad_y = grad_out.astype(jnp.float32)
    grad_filtered = (grad_y * query_feat.astype(jnp.float32)).astype(jnp.bfloat16)
    grad_product = later_sum(grad_filtered, long_taps)
    grad_featured = jnp.stack([(grad_y * filtered).astype(jnp.bfloat16), (grad_product * value_feat.astype(jnp.float32)).astype(jnp.bfloat16), (grad_product * key_feat.astype(jnp.float32)).astype(jnp.bfloat16)])
    grad_features = jnp.stack([later_sum(grad_featured[i], short_filter[i]).astype(jnp.bfloat16) for i in range(3)])
    grad_short = jnp.stack([lag_products(grad_featured[i], features[i], L_SE) for i in range(3)]) / math.sqrt(TOKENS)
    long_terms = lag_products(grad_filtered, product, L_MR)
    grad_long = long_terms.reshape(L_MR, D // GROUPS, GROUPS).sum(axis=1).T / math.sqrt(TOKENS * GROUP)
    return (grad_features, grad_short, grad_long)
```

```python
import functools
import math

import jax
import jax.numpy as jnp
import ml_dtypes
import numpy as np
from jax import lax
from jax.experimental import pallas as pl
from jax.experimental.pallas import tpu as pltpu
from jax.sharding import PartitionSpec as P

MESH = pl.DeviceIdType.MESH
BF = jnp.bfloat16
F32 = jnp.float32
ROWS = 256
TAPS = 128
SHORT = 7
GROUPS = 256
N = ROWS + TAPS
HALF = N // 2


def split(matrix):
    high = matrix.astype(ml_dtypes.bfloat16)
    low = (matrix - high.astype(np.float64)).astype(ml_dtypes.bfloat16)
    return high, low


def transforms():
    angle = 2 * np.pi * (np.arange(HALF) + 0.5) / N

    def rows(tokens):
        phase = np.outer(angle, tokens)
        return np.concatenate([np.cos(phase), -np.sin(phase)], axis=0)

    local = rows(np.arange(ROWS))
    behind = rows(np.arange(-TAPS, 0))
    forward = np.concatenate([*split(local), *split(behind)], axis=1)
    inverse = np.concatenate(split(local.T / HALF), axis=1)
    return forward, inverse


def kernel(
    dims,
    feat,
    short,
    long,
    gout,
    fwd,
    inv,
    out,
    gs_out,
    gl_out,
    fb,
    gob,
    fwdv,
    invv,
    shortv,
    longv,
    coef,
    xf,
    kb,
    vb,
    prod,
    gfil,
    xhalo,
    yhalo,
    fhalo,
    qhead,
    ghead,
    qn,
    hs,
    xs,
    ys,
    rs,
    rsplit,
    shi,
    slo,
    filt,
    gf,
    gsend,
    grecv,
    outv,
    glp,
    glrecv,
    glb,
    glex,
    glmid,
    glex2,
    glfin,
    gsp,
    gscore,
    gsb,
    gsex,
    gsmid,
    gsex2,
    gsfin,
    ld_sem,
    st_sem,
    halo_s,
    halo_r,
    gl_s,
    gl_r,
    gs_s,
    gs_r,
):
    n_seq, n_ch, n_y, n_z, lanes = dims
    tiles = lanes // 128
    chunks = lanes // 256
    halves = tiles // 4
    s = lax.axis_index("seq")
    ch = lax.axis_index("ch")
    core = lax.rem(s, 2)
    z = lax.rem(s // 2, n_z)
    y = s // (2 * n_z)

    def at(yy, zz, cc):
        return (yy * n_z + zz) * 2 + cc

    ahead = {"seq": lax.rem(s + 1, n_seq)}
    behind = {"seq": lax.rem(s + n_seq - 1, n_seq)}
    sibling = {"seq": at(y, z, 1 - core)}
    ys_peers = [{"seq": at(lax.rem(y + d, n_y), z, core)} for d in range(1, n_y)]
    zs_peers = [{"seq": at(y, lax.rem(z + d, n_z), core)} for d in range(1, n_z)]
    n_own = 2 * n_ch
    own = ch * 2 + core
    xc_peers = []
    for d in range(1, n_own):
        o = lax.rem(own + d, n_own)
        xc_peers.append(({"seq": at(y, z, lax.rem(o, 2)), "ch": o // 2}, o))

    barrier = pltpu.get_barrier_semaphore()
    greet = [ahead, behind] + ys_peers + zs_peers + [p for p, _ in xc_peers]
    for p in greet:
        pl.semaphore_signal(barrier, inc=1, device_id=p, device_id_type=MESH)

    def load(src, dst, i):
        c = pltpu.make_async_copy(src, dst, ld_sem.at[i])
        c.start()
        return c

    f_loads, g_loads = [], []
    c_short = load(short, shortv, 2 * tiles)
    for l in range(tiles):
        f_loads.append(load(feat.at[:, :, l * 128 : (l + 1) * 128], fb.at[l], l))
    for l in range(tiles):
        g_loads.append(load(gout.at[:, l * 128 : (l + 1) * 128], gob.at[l], tiles + l))
    c_long = load(long, longv, 2 * tiles + 1)
    c_fwd = load(fwd, fwdv, 2 * tiles + 2)
    c_inv = load(inv, invv, 2 * tiles + 3)

    def remote(src, dst, ssem, rsem, peer):
        c = pltpu.make_async_remote_copy(
            src_ref=src, dst_ref=dst, send_sem=ssem, recv_sem=rsem, device_id=peer, device_id_type=MESH
        )
        c.start()
        return c

    c_short.wait()
    for i in range(3):
        taps = shortv[i].astype(F32)
        for l in range(tiles):
            coef[l, i, 0:SHORT, :] = taps[:, l * 128 : (l + 1) * 128]
    for c in f_loads:
        c.wait()

    def tap(l, i):
        return [coef[l, i, j : j + 1, :] for j in range(SHORT)]

    def fir(ref, l, i, c, first):
        total = c[0] * ref[l, i, first : first + 16, :]
        for j in range(1, SHORT):
            total = total + c[j] * ref[l, i, first - j : first - j + 16, :]
        return total.astype(BF)

    def widen(l, i, lo, hi):
        for r in range(lo, hi, 16):
            xf[l, i, 8 + r : 24 + r, :] = fb[l, i, r : r + 16, :].astype(F32)

    def lane(l):
        return pl.ds(pl.multiple_of(lax.rem(l, 2) * 128, 128), 128)

    def product_rows(l, lo, hi):
        ck, cv = tap(l, 1), tap(l, 2)
        for r in range(lo, hi, 16):
            k = fir(xf, l, 1, ck, 8 + r)
            v = fir(xf, l, 2, cv, 8 + r)
            kb[l, r : r + 16, :] = k
            vb[l, r : r + 16, :] = v
            prod[l // 2, r : r + 16, lane(l)] = (k.astype(F32) * v.astype(F32)).astype(BF)

    def grad_rows(l, lo, hi):
        cq = tap(l, 0)
        for r in range(lo, hi, 16):
            q = fir(xf, l, 0, cq, 8 + r)
            gfil[l // 2, r : r + 16, lane(l)] = (
                q.astype(F32) * gob[l, r : r + 16, :].astype(F32)
            ).astype(BF)

    def tail(l, _):
        widen(l, 1, 112, ROWS)
        widen(l, 2, 112, ROWS)
        product_rows(l, 128, ROWS)
        return 0

    lax.fori_loop(0, tiles, tail, 0)

    pl.semaphore_wait(barrier, len(greet))
    sends = []
    c_fh = remote(feat.at[:, ROWS - 16 :, :], fhalo, halo_s.at[0], halo_r.at[0], ahead)
    c_qh = remote(feat.at[0, 0:16, :], qhead, halo_s.at[1], halo_r.at[1], behind)
    c_gh = remote(gout.at[0:16, :], ghead, halo_s.at[2], halo_r.at[2], behind)
    c_x, c_y, c_g = {}, {}, {}
    for q in range(chunks):
        c_x[q] = remote(
            prod.at[q, ROWS - TAPS :, :], xhalo.at[q], halo_s.at[3 + q], halo_r.at[3 + q], ahead
        )

    for c in g_loads:
        c.wait()

    def head(l, _):
        widen(l, 0, 0, 128)
        grad_rows(l, 16, 128)
        return 0

    order = list(range(chunks // 2, chunks)) + list(range(chunks // 2))
    for q in order:
        lax.fori_loop(2 * q, 2 * q + 2, head, 0)
        i = 3 + chunks + q
        c_y[q] = remote(
            gfil.at[q, 16:TAPS, :], yhalo.at[q, 16:TAPS, :], halo_s.at[i], halo_r.at[i], behind
        )

    def rest(l, _):
        widen(l, 0, 128, ROWS)
        grad_rows(l, 128, ROWS)
        widen(l, 1, 0, 112)
        widen(l, 2, 0, 112)
        product_rows(l, 16, 128)
        return 0

    lax.fori_loop(0, tiles, rest, 0)

    c_long.wait()
    c_fwd.wait()
    nt = (((1,), (1,)), ((), ()))
    hs[...] = lax.dot_general(fwdv[:, 0:TAPS], longv[...], nt, preferred_element_type=F32) + lax.dot_general(
        fwdv[:, ROWS : ROWS + TAPS], longv[...], nt, preferred_element_type=F32
    )

    not_first = jnp.where(s > 0, 1.0, 0.0).astype(F32)
    not_last = jnp.where(s < n_seq - 1, 1.0, 0.0).astype(F32)
    c_fh.wait()
    c_qh.wait()
    c_gh.wait()
    for l in range(tiles):
        cols = slice(l * 128, (l + 1) * 128)
        for i in range(3):
            xf[l, i, 0:8, :] = fhalo[i, :, cols].astype(F32)[8:16] * not_first
        qn[l, 0, 0:8, :] = xf[l, 0, ROWS : ROWS + 8, :]
        qn[l, 0, 8:24, :] = qhead[:, cols].astype(F32)
        product_rows(l, 0, 16)
        grad_rows(l, 0, 16)
        qq = fir(qn, l, 0, tap(l, 0), 8)
        yhalo[l // 2, 0:16, (l % 2) * 128 : (l % 2) * 128 + 128] = (
            qq.astype(F32) * ghead[:, cols].astype(F32)
        ).astype(BF)

    def dot(a, b):
        return jnp.dot(a, b, preferred_element_type=F32)

    def local(q, _):
        p = prod[q]
        xs[q] = dot(fwdv[:, 0:ROWS], p) + dot(fwdv[:, ROWS : 2 * ROWS], p)
        g = gfil[q]
        ys[q] = dot(fwdv[:, 0:ROWS], g) + dot(fwdv[:, ROWS : 2 * ROWS], g)
        return 0

    lax.fori_loop(0, chunks, local, 0)

    def far(h):
        return dot(fwdv[:, 2 * ROWS : 2 * ROWS + TAPS], h) + dot(fwdv[:, 2 * ROWS + TAPS :], h)

    def add_x(q):
        c_x[q].wait()
        xs[q] = xs[q] + not_first * far(xhalo[q])

    def add_y(q):
        c_y[q].wait()
        ys[q] = ys[q] - not_last * far(yhalo[q])

    def corr(q, first):
        def block(b, _):
            re = pl.ds(pl.multiple_of(b * 16, 16), 16)
            im = pl.ds(pl.multiple_of(b * 16 + HALF, 16), 16)
            xr, xi, yr, yi = xs[q, re, :], xs[q, im, :], ys[q, re, :], ys[q, im, :]
            rr = xr * yr + xi * yi
            ri = xr * yi - xi * yr
            if not first:
                rr = rr + rs[re, :]
                ri = ri + rs[im, :]
            rs[re, :] = rr
            rs[im, :] = ri
            return 0

        lax.fori_loop(0, HALF // 16, block, 0)

    def hilo(value):
        high = value.astype(BF)
        return high, (value - high.astype(F32)).astype(BF)

    for q in range(chunks // 2):
        add_x(q)
        corr(q, q == 0)
    for q in range(chunks // 2, chunks):
        add_y(q)
        corr(q, False)
    c_inv.wait()
    rh, rl = hilo(rs[...])
    glp[...] = (
        dot(invv[0:TAPS, 0:N], rh) + dot(invv[0:TAPS, N:], rh) + dot(invv[0:TAPS, 0:N], rl)
    )

    own_rows = TAPS // n_own
    mine = pl.ds(pl.multiple_of(own * own_rows, own_rows), own_rows)
    gl_c = []
    for d, (p, o) in enumerate(xc_peers):
        piece = pl.ds(pl.multiple_of(o * own_rows, own_rows), own_rows)
        gl_c.append(remote(glp.at[piece, :], glrecv.at[d], gl_s.at[0, 0, d], gl_r.at[0, 0, d], p))

    def spread(src, dst, sems, peers):
        ss, rr = sems
        return [remote(src, dst.at[d], ss.at[d], rr.at[d], p) for d, p in enumerate(peers)]

    def gl_one():
        for c in gl_c:
            c.wait()
        total = glp[mine, :]
        for d in range(n_own - 1):
            total = total + glrecv[d]
        res = []
        for k in range(2):
            glb[k] = total[:, k * 128 : (k + 1) * 128].astype(BF)
            peers = ys_peers if k == 0 else zs_peers
            res.append(spread(glb.at[k], glex.at[k], (gl_s.at[1, k], gl_r.at[1, k]), peers))
        return res

    def gl_two(cs):
        res = []
        for k in range(2):
            for c in cs[k]:
                c.wait()
            total = glb[k].astype(F32)
            for d in range(len(cs[k])):
                total = total + glex[k, d].astype(F32)
            glmid[k] = total.astype(BF)
            peers = zs_peers if k == 0 else ys_peers
            res.append(spread(glmid.at[k], glex2.at[k], (gl_s.at[2, k], gl_r.at[2, k]), peers))
        return res

    def gl_three(cs):
        for k in range(2):
            for c in cs[k]:
                c.wait()
            total = glmid[k].astype(F32)
            for d in range(len(cs[k])):
                total = total + glex2[k, d].astype(F32)
            glfin[mine, k * 128 : (k + 1) * 128] = total
        res = []
        for d, (p, _) in enumerate(xc_peers):
            res.append(remote(glfin.at[mine, :], glfin.at[mine, :], gl_s.at[3, 0, d], gl_r.at[3, 0, d], p))
        return res

    def gl_four(cs):
        for c in cs:
            c.wait()
        gl_out[...] = glfin[...].T

    def gs_zero(h):
        theirs = pl.ds(4 * h + 2 * (1 - core), 2)
        return remote(gsp.at[theirs], gscore.at[h], gs_s.at[h, 0, 0], gs_r.at[h, 0, 0], sibling)

    def gs_one(h, c):
        c.wait()
        total = gsp[pl.ds(4 * h + 2 * core, 2)] + gscore[h]
        gsb[h] = total.reshape(48, 128).astype(BF)
        peers = ys_peers if h % 2 == 0 else zs_peers
        return spread(gsb.at[h], gsex.at[h], (gs_s.at[h, 1], gs_r.at[h, 1]), peers)

    def gs_two(h, cs):
        for c in cs:
            c.wait()
        total = gsb[h].astype(F32)
        for d in range(len(cs)):
            total = total + gsex[h, d].astype(F32)
        gsmid[h] = total.astype(BF)
        peers = zs_peers if h % 2 == 0 else ys_peers
        return spread(gsmid.at[h], gsex2.at[h], (gs_s.at[h, 2], gs_r.at[h, 2]), peers)

    def gs_three(h, cs):
        for c in cs:
            c.wait()
        total = gsmid[h].astype(F32)
        for d in range(len(cs)):
            total = total + gsex2[h, d].astype(F32)
        here = pl.ds(4 * h + 2 * core, 2)
        gsfin[here] = total.reshape(2, 24, 128)
        return remote(gsfin.at[here], gsfin.at[here], gs_s.at[h, 3, 0], gs_r.at[h, 3, 0], sibling)

    def gs_four(h, c):
        c.wait()
        for l in range(4 * h, 4 * h + 4):
            for i in range(3):
                gs_out[i, :, l * 128 : (l + 1) * 128] = gsfin[l, 8 * i : 8 * i + 8, :]

    def spectra(q):
        def block(b, _):
            re = pl.ds(pl.multiple_of(b * 16, 16), 16)
            im = pl.ds(pl.multiple_of(b * 16 + HALF, 16), 16)
            hr, hi = hs[re, :], hs[im, :]
            xr, xi = xs[q, re, :], xs[q, im, :]
            yr, yi = ys[q, re, :], ys[q, im, :]
            parts = (
                (re, 0, xr * hr - xi * hi),
                (im, 0, xr * hi + xi * hr),
                (re, 256, yr * hr + yi * hi),
                (im, 256, yi * hr - yr * hi),
            )
            for rows, c, value in parts:
                high, low = hilo(value)
                shi[rows, c : c + 256] = high
                slo[rows, c : c + 256] = low
            return 0

        lax.fori_loop(0, HALF // 16, block, 0)
        for c in (0, 256):
            sh = shi[:, c : c + 256]
            filt[:, c : c + 256] = (
                dot(invv[:, 0:N], sh) + dot(invv[:, N:], sh) + dot(invv[:, 0:N], slo[:, c : c + 256])
            )

    def featured_grad(l, h):
        for r in range(0, ROWS, 16):
            rows = slice(r, r + 16)
            fa = filt[rows, h * 128 : h * 128 + 128]
            fg = filt[rows, 256 + h * 128 : 256 + h * 128 + 128]
            g0 = (gob[l, rows, :].astype(F32) * fa).astype(BF)
            g1 = (fg * vb[l, rows, :].astype(F32)).astype(BF)
            g2 = (fg * kb[l, rows, :].astype(F32)).astype(BF)
            for i, g in enumerate((g0, g1, g2)):
                gf[l, i, rows, :] = g.astype(F32)
                if r == 0:
                    gsend[l, i] = g

    def short_grad(l):
        for i in range(3):
            acc = [jnp.zeros((8, 128), F32) for _ in range(SHORT)]
            for r in range(0, ROWS, 8):
                g = gf[l, i, r : r + 8, :]
                for j in range(SHORT):
                    acc[j] = acc[j] + g * xf[l, i, 8 + r - j : 16 + r - j, :]
            rows = [jnp.sum(a, axis=0, keepdims=True) for a in acc]
            rows.append(jnp.zeros((1, 128), F32))
            gsp[l, 8 * i : 8 * i + 8, :] = jnp.concatenate(rows, axis=0)

    def chunk(q):
        if q < chunks // 2:
            add_y(q)
        else:
            add_x(q)
        spectra(q)
        for h in range(2):
            featured_grad(2 * q + h, h)
        i = 3 + 2 * chunks + q
        two = pl.ds(2 * q, 2)
        c_g[q] = remote(gsend.at[two], grecv.at[two], halo_s.at[i], halo_r.at[i], behind)

        def sg(l, _):
            short_grad(l)
            return 0

        lax.fori_loop(2 * q, 2 * q + 2, sg, 0)

    def conv(q):
        c_g[q].wait()

        def one(l, _):
            for i in range(3):
                gf[l, i, ROWS : ROWS + 8, :] = grecv[l, i].astype(F32)[0:8] * not_last
                c = tap(l, i)
                for r in range(0, ROWS, 16):
                    total = c[0] * gf[l, i, r : r + 16, :]
                    for j in range(1, SHORT):
                        total = total + c[j] * gf[l, i, r + j : r + j + 16, :]
                    outv[l, i, r : r + 16, :] = total.astype(BF)
            return 0

        lax.fori_loop(2 * q, 2 * q + 2, one, 0)
        res = []
        for l in (2 * q, 2 * q + 1):
            c = pltpu.make_async_copy(outv.at[l], out.at[:, :, l * 128 : (l + 1) * 128], st_sem.at[l])
            c.start()
            res.append(c)
        return res

    stores = []
    chunk(0)
    chunk(1)
    a0 = gs_zero(0)
    chunk(2)
    gl1 = gl_one()
    a1 = gs_one(0, a0)
    chunk(3)
    b0 = gs_zero(1)
    gl2 = gl_two(gl1)
    stores += conv(0)
    b1 = gs_one(1, b0)
    a2 = gs_two(0, a1)
    stores += conv(1)
    gl3 = gl_three(gl2)
    b2 = gs_two(1, b1)
    stores += conv(2)
    a3 = gs_three(0, a2)
    stores += conv(3)
    b3 = gs_three(1, b2)
    gs_four(0, a3)
    gl_four(gl3)
    gs_four(1, b3)
    for c in stores:
        c.wait()


def solution(mesh):
    n_seq, n_ch = mesh.shape["seq"], mesh.shape["ch"]
    n_z = math.isqrt(n_seq // 2)
    n_y = n_seq // (2 * n_z)
    forward, inverse = transforms()

    def body(features, short_filter, long_filter, grad_out):
        lanes = features.shape[2]
        tiles, chunks, halves = lanes // 128, lanes // 256, lanes // 512
        n_own = 2 * n_ch
        own_rows = TAPS // n_own
        most = max(n_y, n_z, n_own)
        any_spec = pl.BlockSpec(memory_space=pl.ANY)
        vmem = pl.BlockSpec(memory_space=pltpu.VMEM)
        V = pltpu.VMEM
        D = pltpu.SemaphoreType.DMA
        grad_features, grad_short, grad_long = pl.pallas_call(
            functools.partial(kernel, (n_seq, n_ch, n_y, n_z, lanes)),
            out_shape=(
                jax.ShapeDtypeStruct((3, ROWS, lanes), BF),
                jax.ShapeDtypeStruct((3, 8, lanes), F32),
                jax.ShapeDtypeStruct((GROUPS, TAPS), F32),
            ),
            in_specs=[any_spec] * 6,
            out_specs=(any_spec, vmem, vmem),
            scratch_shapes=[
                V((tiles, 3, ROWS, 128), BF),
                V((tiles, ROWS, 128), BF),
                V((N, 2 * N), BF),
                V((ROWS, 2 * N), BF),
                V((3, SHORT, lanes), BF),
                V((GROUPS, TAPS), BF),
                V((tiles, 3, 8, 128), F32),
                V((tiles, 3, ROWS + 8, 128), F32),
                V((tiles, ROWS, 128), BF),
                V((tiles, ROWS, 128), BF),
                V((chunks, ROWS, 256), BF),
                V((chunks, ROWS, 256), BF),
                V((chunks, TAPS, 256), BF),
                V((chunks, TAPS, 256), BF),
                V((3, 16, lanes), BF),
                V((16, lanes), BF),
                V((16, lanes), BF),
                V((tiles, 1, 24, 128), F32),
                V((N, 256), F32),
                V((chunks, N, 256), F32),
                V((chunks, N, 256), F32),
                V((N, 256), F32),
                V((2, N, 256), BF),
                V((N, 512), BF),
                V((N, 512), BF),
                V((ROWS, 512), F32),
                V((tiles, 3, ROWS + 8, 128), F32),
                V((tiles, 3, 16, 128), BF),
                V((tiles, 3, 16, 128), BF),
                V((tiles, 3, ROWS, 128), BF),
                V((TAPS, 256), F32),
                V((n_own - 1, own_rows, 256), F32),
                V((2, own_rows, 128), BF),
                V((2, most - 1, own_rows, 128), BF),
                V((2, own_rows, 128), BF),
                V((2, most - 1, own_rows, 128), BF),
                V((TAPS, 256), F32),
                V((tiles, 24, 128), F32),
                V((halves, 2, 24, 128), F32),
                V((halves, 48, 128), BF),
                V((halves, most - 1, 48, 128), BF),
                V((halves, 48, 128), BF),
                V((halves, most - 1, 48, 128), BF),
                V((tiles, 24, 128), F32),
                D((2 * tiles + 4,)),
                D((tiles,)),
                D((3 + 3 * chunks,)),
                D((3 + 3 * chunks,)),
                D((4, 2, most)),
                D((4, 2, most)),
                D((halves, 4, most)),
                D((halves, 4, most)),
            ],
            compiler_params=pltpu.CompilerParams(
                collective_id=0, has_side_effects=True, vmem_limit_bytes=56 * 2**20
            ),
            name="hyena_backward",
        )(features, short_filter, long_filter, grad_out, jnp.asarray(forward), jnp.asarray(inverse))
        tokens = ROWS * n_seq
        grad_short = grad_short[:, :SHORT, :] / math.sqrt(tokens)
        grad_long = grad_long / math.sqrt(tokens * (lanes * n_ch // GROUPS))
        return grad_features, grad_short, grad_long

    return jax.shard_map(
        body,
        mesh=mesh,
        in_specs=(P(None, "seq", "ch"), P(None, None, "ch"), P(), P("seq", "ch")),
        out_specs=(P(None, "seq", "ch"), P(None, None, "ch"), P()),
        check_vma=False,
    )
```

```python
import functools
import math

import jax
import jax.numpy as jnp
import ml_dtypes
import numpy as np
from jax import lax
from jax.experimental import pallas as pl
from jax.experimental.pallas import tpu as pltpu
from jax.sharding import PartitionSpec as P

MESH = pl.DeviceIdType.MESH
BF = jnp.bfloat16
F32 = jnp.float32
ROWS = 256
TAPS = 128
SHORT = 7
GROUPS = 256
N = ROWS + TAPS
HALF = N // 2


def split(matrix):
    high = matrix.astype(ml_dtypes.bfloat16)
    low = (matrix - high.astype(np.float64)).astype(ml_dtypes.bfloat16)
    return high, low


def transforms():
    angle = 2 * np.pi * (np.arange(HALF) + 0.5) / N

    def rows(tokens):
        phase = np.outer(angle, tokens)
        return np.concatenate([np.cos(phase), -np.sin(phase)], axis=0)

    local = rows(np.arange(ROWS))
    behind = rows(np.arange(-TAPS, 0))
    forward = np.concatenate([*split(local), *split(behind)], axis=1)
    inverse = np.concatenate(split(local.T / HALF), axis=1)
    return forward, inverse


def kernel(
    dims,
    feat,
    short,
    long,
    gout,
    fwd,
    inv,
    out,
    gs_out,
    gl_out,
    fb,
    gob,
    fwdv,
    invv,
    shortv,
    longv,
    coef,
    xf,
    kb,
    vb,
    prod,
    gfil,
    xhalo,
    yhalo,
    raw,
    qn,
    hs,
    xs,
    ys,
    rs,
    shi,
    slo,
    filt,
    gf,
    gsend,
    grecv,
    glp,
    glrecv,
    glb,
    glex,
    glmid,
    glex2,
    glfin,
    gsp,
    gscore,
    gsb,
    gsex,
    gsmid,
    gsex2,
    gsfin,
    ld_sem,
    halo_s,
    raw_r,
    x_r,
    y_r,
    g_r,
    gl_s,
    gl_r,
    gs_s,
    gs_r,
):
    n_seq, n_ch, n_y, n_z, lanes = dims
    tokens = ROWS * n_seq
    gs_scale = 1.0 / math.sqrt(tokens)
    gl_scale = 1.0 / math.sqrt(tokens * (lanes * n_ch // GROUPS))
    tiles = lanes // 128
    chunks = lanes // 256
    halves = tiles // 4
    s = lax.axis_index("seq")
    ch = lax.axis_index("ch")
    core = lax.rem(s, 2)
    z = lax.rem(s // 2, n_z)
    y = s // (2 * n_z)

    def at(yy, zz, cc):
        return (yy * n_z + zz) * 2 + cc

    ahead = {"seq": lax.rem(s + 1, n_seq)}
    behind = {"seq": lax.rem(s + n_seq - 1, n_seq)}
    sibling = {"seq": at(y, z, 1 - core)}
    ys_peers = [{"seq": at(lax.rem(y + d, n_y), z, core)} for d in range(1, n_y)]
    zs_peers = [{"seq": at(y, lax.rem(z + d, n_z), core)} for d in range(1, n_z)]
    n_own = 2 * n_ch
    own = ch * 2 + core
    xc_peers = []
    for d in range(1, n_own):
        o = lax.rem(own + d, n_own)
        xc_peers.append(({"seq": at(y, z, lax.rem(o, 2)), "ch": o // 2}, o))

    barrier = pltpu.get_barrier_semaphore()
    greet = [ahead, behind] + ys_peers + zs_peers + [p for p, _ in xc_peers]
    for p in greet:
        pl.semaphore_signal(barrier, inc=1, device_id=p, device_id_type=MESH)

    def load(src, dst, i):
        c = pltpu.make_async_copy(src, dst, ld_sem.at[i])
        c.start()
        return c

    def all_of(ref, sem):
        pltpu.make_async_copy(ref, ref, sem).wait()

    c_short = load(short, shortv, 0)
    for l in range(tiles):
        load(feat.at[:, :, l * 128 : (l + 1) * 128], fb.at[l], 1)
    for l in range(tiles):
        load(gout.at[:, l * 128 : (l + 1) * 128], gob.at[l], 2)
    c_long = load(long, longv, 3)
    c_fwd = load(fwd, fwdv, 4)
    c_inv = load(inv, invv, 5)

    def remote(src, dst, ssem, rsem, peer):
        pltpu.make_async_remote_copy(
            src_ref=src, dst_ref=dst, send_sem=ssem, recv_sem=rsem, device_id=peer, device_id_type=MESH
        ).start()

    c_short.wait()
    for i in range(3):
        taps = shortv[i].astype(F32)
        for l in range(tiles):
            coef[l, i, 0:SHORT, :] = taps[:, l * 128 : (l + 1) * 128]
    all_of(fb, ld_sem.at[1])

    def tap(l, i):
        return [coef[l, i, j : j + 1, :] for j in range(SHORT)]

    def fir(ref, l, i, c, first):
        total = c[0] * ref[l, i, first : first + 16, :]
        for j in range(1, SHORT):
            total = total + c[j] * ref[l, i, first - j : first - j + 16, :]
        return total.astype(BF)

    def widen(l, i, lo, hi):
        for r in range(lo, hi, 16):
            xf[l, i, 8 + r : 24 + r, :] = fb[l, i, r : r + 16, :].astype(F32)

    def tile(l):
        return pl.ds(pl.multiple_of(l * 128, 128), 128)

    def lane(l):
        return pl.ds(pl.multiple_of(lax.rem(l, 2) * 128, 128), 128)

    def product_rows(l, lo, hi):
        ck, cv = tap(l, 1), tap(l, 2)
        for r in range(lo, hi, 16):
            k = fir(xf, l, 1, ck, 8 + r)
            v = fir(xf, l, 2, cv, 8 + r)
            kb[l, r : r + 16, :] = k
            vb[l, r : r + 16, :] = v
            prod[l // 2, r : r + 16, lane(l)] = (k.astype(F32) * v.astype(F32)).astype(BF)

    def grad_rows(l, lo, hi):
        cq = tap(l, 0)
        for r in range(lo, hi, 16):
            q = fir(xf, l, 0, cq, 8 + r)
            gfil[l // 2, r : r + 16, lane(l)] = (
                q.astype(F32) * gob[l, r : r + 16, :].astype(F32)
            ).astype(BF)

    def tail(l, _):
        widen(l, 1, 112, ROWS)
        widen(l, 2, 112, ROWS)
        product_rows(l, 128, ROWS)
        return 0

    def tails():
        lax.fori_loop(0, tiles, tail, 0)

    raw_s, x_s, y_s, g_s = (halo_s.at[k] for k in range(4))

    def send_first():
        pl.semaphore_wait(barrier, len(greet))
        remote(feat.at[:, ROWS - 16 :, :], raw.at[0:3], raw_s, raw_r.at[0], ahead)
        remote(feat.at[0, 0:16, :], raw.at[3], raw_s, raw_r.at[0], behind)
        remote(gout.at[0:16, :], raw.at[4], raw_s, raw_r.at[0], behind)
        for q in range(chunks):
            remote(prod.at[q, ROWS - TAPS :, :], xhalo.at[q], x_s, x_r.at[q], ahead)

    def head(l, _):
        widen(l, 0, 0, 128)
        grad_rows(l, 16, 128)
        return 0

    def heads(q):
        lax.fori_loop(2 * q, 2 * q + 2, head, 0)

    def send_head(q):
        remote(gfil.at[q, 16:TAPS, :], yhalo.at[q, 16:TAPS, :], y_s, y_r.at[q], behind)

    def rest(l, _):
        widen(l, 0, 128, ROWS)
        grad_rows(l, 128, ROWS)
        widen(l, 1, 0, 112)
        widen(l, 2, 0, 112)
        product_rows(l, 16, 128)
        return 0

    def rests():
        lax.fori_loop(0, tiles, rest, 0)

    nt = (((1,), (1,)), ((), ()))

    def spectrum():
        hs[...] = lax.dot_general(fwdv[:, 0:TAPS], longv[...], nt, preferred_element_type=F32) + lax.dot_general(
        fwdv[:, ROWS : ROWS + TAPS], longv[...], nt, preferred_element_type=F32
    )

    not_first = jnp.where(s > 0, 1.0, 0.0).astype(F32)
    not_last = jnp.where(s < n_seq - 1, 1.0, 0.0).astype(F32)
    def edges(l):
        cols = slice(l * 128, (l + 1) * 128)
        for i in range(3):
            xf[l, i, 0:8, :] = raw[i, :, cols].astype(F32)[8:16] * not_first
        qn[l, 0, 0:8, :] = xf[l, 0, ROWS : ROWS + 8, :]
        qn[l, 0, 8:24, :] = raw[3, :, cols].astype(F32)
        product_rows(l, 0, 16)
        grad_rows(l, 0, 16)
        qq = fir(qn, l, 0, tap(l, 0), 8)
        yhalo[l // 2, 0:16, (l % 2) * 128 : (l % 2) * 128 + 128] = (
            qq.astype(F32) * raw[4, :, cols].astype(F32)
        ).astype(BF)

    def dot(a, b):
        return jnp.dot(a, b, preferred_element_type=F32)

    def local(q):
        p = prod[q]
        xs[q] = dot(fwdv[:, 0:ROWS], p) + dot(fwdv[:, ROWS : 2 * ROWS], p)
        g = gfil[q]
        ys[q] = dot(fwdv[:, 0:ROWS], g) + dot(fwdv[:, ROWS : 2 * ROWS], g)


    def far(h):
        return dot(fwdv[:, 2 * ROWS : 2 * ROWS + TAPS], h) + dot(fwdv[:, 2 * ROWS + TAPS :], h)

    def wait_x(q):
        all_of(xhalo.at[q], x_r.at[q])

    def wait_y(q):
        all_of(yhalo.at[q, 16:TAPS, :], y_r.at[q])

    def add_x(q):
        wait_x(q)
        xs[q] = xs[q] + not_first * far(xhalo[q])

    def add_y(q):
        wait_y(q)
        ys[q] = ys[q] - not_last * far(yhalo[q])

    def corr(q, first):
        def block(b, _):
            re = pl.ds(pl.multiple_of(b * 16, 16), 16)
            im = pl.ds(pl.multiple_of(b * 16 + HALF, 16), 16)
            xr, xi, yr, yi = xs[q, re, :], xs[q, im, :], ys[q, re, :], ys[q, im, :]
            rr = xr * yr + xi * yi
            ri = xr * yi - xi * yr
            if not first:
                rr = rr + rs[re, :]
                ri = ri + rs[im, :]
            rs[re, :] = rr
            rs[im, :] = ri
            return 0

        lax.fori_loop(0, HALF // 16, block, 0)

    def hilo(value):
        high = value.astype(BF)
        return high, (value - high.astype(F32)).astype(BF)

    def lags():
        rh, rl = hilo(rs[...])
        glp[...] = (
            dot(invv[0:TAPS, 0:N], rh) + dot(invv[0:TAPS, N:], rh) + dot(invv[0:TAPS, 0:N], rl)
        )

    own_rows = TAPS // n_own
    mine = pl.ds(pl.multiple_of(own * own_rows, own_rows), own_rows)

    def gl_zero():
        for d, (p, o) in enumerate(xc_peers):
            piece = pl.ds(pl.multiple_of(o * own_rows, own_rows), own_rows)
            remote(glp.at[piece, :], glrecv.at[d], gl_s.at[0], gl_r.at[0], p)

    def spread(src, dst, ssem, rsem, peers):
        for d, p in enumerate(peers):
            remote(src, dst.at[d], ssem, rsem, p)

    def gathered(mid, ref, sem, peers):
        all_of(ref.at[0 : len(peers)], sem)
        total = mid.astype(F32)
        for d in range(len(peers)):
            total = total + ref[d].astype(F32)
        return total

    rings = ((ys_peers, zs_peers), (zs_peers, ys_peers))

    def gl_one():
        total = gathered(glp[mine, :], glrecv, gl_r.at[0], xc_peers)
        for k in range(2):
            glb[k] = total[:, k * 128 : (k + 1) * 128].astype(BF)
            spread(glb.at[k], glex.at[k], gl_s.at[1 + k], gl_r.at[1 + k], rings[k][0])

    def gl_two():
        for k in range(2):
            glmid[k] = gathered(glb[k], glex.at[k], gl_r.at[1 + k], rings[k][0]).astype(BF)
            spread(glmid.at[k], glex2.at[k], gl_s.at[3 + k], gl_r.at[3 + k], rings[k][1])

    def gl_three():
        for k in range(2):
            total = gathered(glmid[k], glex2.at[k], gl_r.at[3 + k], rings[k][1])
            glfin[mine, k * 128 : (k + 1) * 128] = total * gl_scale
        for d, (p, _) in enumerate(xc_peers):
            remote(glfin.at[mine, :], glfin.at[mine, :], gl_s.at[5], gl_r.at[5], p)

    def gl_four():
        all_of(glfin.at[0 : TAPS - own_rows], gl_r.at[5])
        gl_out[...] = glfin[...].T

    def gs_zero(h):
        theirs = pl.ds(4 * h + 2 * (1 - core), 2)
        remote(gsp.at[theirs], gscore.at[h], gs_s.at[h, 0], gs_r.at[h, 0], sibling)

    def gs_one(h):
        all_of(gscore.at[h], gs_r.at[h, 0])
        total = gsp[pl.ds(4 * h + 2 * core, 2)] + gscore[h]
        gsb[h] = total.reshape(48, 128).astype(BF)
        spread(gsb.at[h], gsex.at[h], gs_s.at[h, 1], gs_r.at[h, 1], rings[h % 2][0])

    def gs_two(h):
        gsmid[h] = gathered(gsb[h], gsex.at[h], gs_r.at[h, 1], rings[h % 2][0]).astype(BF)
        spread(gsmid.at[h], gsex2.at[h], gs_s.at[h, 2], gs_r.at[h, 2], rings[h % 2][1])

    def gs_three(h):
        total = gathered(gsmid[h], gsex2.at[h], gs_r.at[h, 2], rings[h % 2][1]) * gs_scale
        here = pl.ds(4 * h + 2 * core, 2)
        gsfin[here] = total.reshape(2, 24, 128)
        remote(gsfin.at[here], gsfin.at[here], gs_s.at[h, 3], gs_r.at[h, 3], sibling)

    def gs_four(h):
        all_of(gscore.at[h], gs_r.at[h, 3])
        for l in range(4 * h, 4 * h + 4):
            for i in range(3):
                gs_out[i, :, l * 128 : (l + 1) * 128] = gsfin[l, 8 * i : 8 * i + SHORT, :]

    def spectra(q):
        def block(b, _):
            re = pl.ds(pl.multiple_of(b * 16, 16), 16)
            im = pl.ds(pl.multiple_of(b * 16 + HALF, 16), 16)
            hr, hi = hs[re, :], hs[im, :]
            xr, xi = xs[q, re, :], xs[q, im, :]
            yr, yi = ys[q, re, :], ys[q, im, :]
            parts = (
                (re, 0, xr * hr - xi * hi),
                (im, 0, xr * hi + xi * hr),
                (re, 256, yr * hr + yi * hi),
                (im, 256, yi * hr - yr * hi),
            )
            for rows, c, value in parts:
                high, low = hilo(value)
                shi[rows, c : c + 256] = high
                slo[rows, c : c + 256] = low
            return 0

        lax.fori_loop(0, HALF // 16, block, 0)

    def inverse():
        for c in (0, 256):
            sh = shi[:, c : c + 256]
            filt[:, c : c + 256] = (
                dot(invv[:, 0:N], sh) + dot(invv[:, N:], sh) + dot(invv[:, 0:N], slo[:, c : c + 256])
            )

    def featured_grad(l, h):
        for r in range(0, ROWS, 16):
            rows = slice(r, r + 16)
            fa = filt[rows, h * 128 : h * 128 + 128]
            fg = filt[rows, 256 + h * 128 : 256 + h * 128 + 128]
            g0 = (gob[l, rows, :].astype(F32) * fa).astype(BF)
            g1 = (fg * vb[l, rows, :].astype(F32)).astype(BF)
            g2 = (fg * kb[l, rows, :].astype(F32)).astype(BF)
            for i, g in enumerate((g0, g1, g2)):
                gf[l, i, rows, :] = g.astype(F32)
                if r == 0:
                    gsend[l, i] = g

    def short_grad(l):
        for i in range(3):
            acc = [jnp.zeros((8, 128), F32) for _ in range(SHORT)]
            for r in range(0, ROWS, 8):
                g = gf[l, i, r : r + 8, :]
                for j in range(SHORT):
                    acc[j] = acc[j] + g * xf[l, i, 8 + r - j : 16 + r - j, :]
            rows = [jnp.sum(a, axis=0, keepdims=True) for a in acc]
            rows.append(jnp.zeros((1, 128), F32))
            gsp[l, 8 * i : 8 * i + 8, :] = jnp.concatenate(rows, axis=0)

    def fgrads(q):
        for h in range(2):
            featured_grad(2 * q + h, h)

    def send_grad(q):
        two = pl.ds(2 * q, 2)
        remote(gsend.at[two], grecv.at[two], g_s, g_r.at[q], behind)

    def sgrads(q):
        def sg(l, _):
            short_grad(l)
            return 0

        lax.fori_loop(2 * q, 2 * q + 2, sg, 0)

    def wait_grad(q):
        all_of(grecv.at[pl.ds(2 * q, 2)], g_r.at[q])

    def conv(q):
        wait_grad(q)

        def one(l, _):
            for i in range(3):
                gf[l, i, ROWS : ROWS + 8, :] = grecv[l, i].astype(F32)[0:8] * not_last
                c = tap(l, i)
                for r in range(0, ROWS, 16):
                    total = c[0] * gf[l, i, r : r + 16, :]
                    for j in range(1, SHORT):
                        total = total + c[j] * gf[l, i, r + j : r + j + 16, :]
                    out[i, r : r + 16, tile(l)] = total.astype(BF)
            return 0

        lax.fori_loop(2 * q, 2 * q + 2, one, 0)

    tails()
    send_first()
    all_of(gob, ld_sem.at[2])
    order = list(range(chunks // 2, chunks)) + list(range(chunks // 2))
    for q in order:
        heads(q)
        send_head(q)
    rests()
    c_long.wait()
    c_fwd.wait()
    spectrum()
    all_of(raw, raw_r.at[0])
    for l in range(tiles):
        edges(l)
    for q in range(chunks):
        local(q)
    for q in range(chunks // 2):
        add_x(q)
        corr(q, q == 0)
    for q in range(chunks // 2, chunks):
        add_y(q)
        corr(q, False)
    c_inv.wait()
    lags()
    gl_zero()

    def chunk(q):
        if q < chunks // 2:
            add_y(q)
        else:
            add_x(q)
        spectra(q)
        inverse()
        fgrads(q)
        send_grad(q)
        sgrads(q)

    chunk(0)
    chunk(1)
    gs_zero(0)
    chunk(2)
    gl_one()
    gs_one(0)
    chunk(3)
    gs_zero(1)
    gl_two()
    conv(0)
    gs_one(1)
    gs_two(0)
    conv(1)
    gl_three()
    gs_two(1)
    conv(2)
    gs_three(0)
    conv(3)
    gs_three(1)
    gs_four(0)
    gl_four()
    gs_four(1)

    all_of(raw, raw_s)
    all_of(xhalo, x_s)
    all_of(yhalo.at[:, 16:TAPS, :], y_s)
    all_of(grecv, g_s)
    all_of(glrecv, gl_s.at[0])
    for k in range(2):
        all_of(glex.at[k, 0 : len(rings[k][0])], gl_s.at[1 + k])
        all_of(glex2.at[k, 0 : len(rings[k][1])], gl_s.at[3 + k])
    all_of(glrecv, gl_s.at[5])
    for h in range(halves):
        all_of(gscore.at[h], gs_s.at[h, 0])
        all_of(gsex.at[h, 0 : len(rings[h % 2][0])], gs_s.at[h, 1])
        all_of(gsex2.at[h, 0 : len(rings[h % 2][1])], gs_s.at[h, 2])
        all_of(gscore.at[h], gs_s.at[h, 3])


def solution(mesh):
    n_seq, n_ch = mesh.shape["seq"], mesh.shape["ch"]
    n_z = math.isqrt(n_seq // 2)
    n_y = n_seq // (2 * n_z)
    forward, inverse = transforms()

    def body(features, short_filter, long_filter, grad_out):
        lanes = features.shape[2]
        tiles, chunks, halves = lanes // 128, lanes // 256, lanes // 512
        n_own = 2 * n_ch
        own_rows = TAPS // n_own
        most = max(n_y, n_z)
        any_spec = pl.BlockSpec(memory_space=pltpu.HBM)
        vmem = pl.BlockSpec(memory_space=pltpu.VMEM)
        V = pltpu.VMEM
        D = pltpu.SemaphoreType.DMA
        grad_features, grad_short, grad_long = pl.pallas_call(
            functools.partial(kernel, (n_seq, n_ch, n_y, n_z, lanes)),
            out_shape=(
                V((3, ROWS, lanes), BF),
                V((3, SHORT, lanes), F32),
                V((GROUPS, TAPS), F32),
            ),
            in_specs=[any_spec] * 6,
            out_specs=(vmem, vmem, vmem),
            scratch_shapes=[
                V((tiles, 3, ROWS, 128), BF),
                V((tiles, ROWS, 128), BF),
                V((N, 2 * N), BF),
                V((ROWS, 2 * N), BF),
                V((3, SHORT, lanes), BF),
                V((GROUPS, TAPS), BF),
                V((tiles, 3, 8, 128), F32),
                V((tiles, 3, ROWS + 8, 128), F32),
                V((tiles, ROWS, 128), BF),
                V((tiles, ROWS, 128), BF),
                V((chunks, ROWS, 256), BF),
                V((chunks, ROWS, 256), BF),
                V((chunks, TAPS, 256), BF),
                V((chunks, TAPS, 256), BF),
                V((5, 16, lanes), BF),
                V((tiles, 1, 24, 128), F32),
                V((N, 256), F32),
                V((chunks, N, 256), F32),
                V((chunks, N, 256), F32),
                V((N, 256), F32),
                V((N, 512), BF),
                V((N, 512), BF),
                V((ROWS, 512), F32),
                V((tiles, 3, ROWS + 8, 128), F32),
                V((tiles, 3, 16, 128), BF),
                V((tiles, 3, 16, 128), BF),
                V((TAPS, 256), F32),
                V((n_own - 1, own_rows, 256), F32),
                V((2, own_rows, 128), BF),
                V((2, most - 1, own_rows, 128), BF),
                V((2, own_rows, 128), BF),
                V((2, most - 1, own_rows, 128), BF),
                V((TAPS, 256), F32),
                V((tiles, 24, 128), F32),
                V((halves, 2, 24, 128), F32),
                V((halves, 48, 128), BF),
                V((halves, most - 1, 48, 128), BF),
                V((halves, 48, 128), BF),
                V((halves, most - 1, 48, 128), BF),
                V((tiles, 24, 128), F32),
                D((6,)),
                D((4,)),
                D((1,)),
                D((chunks,)),
                D((chunks,)),
                D((chunks,)),
                D((6,)),
                D((6,)),
                D((halves, 4)),
                D((halves, 4)),
            ],
            compiler_params=pltpu.CompilerParams(
                collective_id=0, has_side_effects=True, vmem_limit_bytes=40 * 2**20
            ),
            name="hyena_backward",
        )(
            *(
                pltpu.with_memory_space_constraint(a, pltpu.HBM)
                for a in (features, short_filter, long_filter, grad_out, jnp.asarray(forward), jnp.asarray(inverse))
            )
        )
        return grad_features, grad_short, grad_long

    return jax.shard_map(
        body,
        mesh=mesh,
        in_specs=(P(None, "seq", "ch"), P(None, None, "ch"), P(), P("seq", "ch")),
        out_specs=(P(None, "seq", "ch"), P(None, None, "ch"), P()),
        check_vma=False,
    )
```

```python
import functools
import math

import jax
import jax.numpy as jnp
import ml_dtypes
import numpy as np
from jax import lax
from jax.experimental import pallas as pl
from jax.experimental.pallas import tpu as pltpu
from jax.sharding import PartitionSpec as P

MESH = pl.DeviceIdType.MESH
BF = jnp.bfloat16
F32 = jnp.float32
ROWS = 256
TAPS = 128
SHORT = 7
EDGE = SHORT - 1
GROUPS = 256
N = ROWS + TAPS
HALF = N // 2


def split(matrix):
    high = matrix.astype(ml_dtypes.bfloat16)
    low = (matrix - high.astype(np.float64)).astype(ml_dtypes.bfloat16)
    return high, low


def transforms():
    angle = 2 * np.pi * (np.arange(HALF) + 0.5) / N

    def rows(tokens):
        phase = np.outer(angle, tokens)
        return np.concatenate([np.cos(phase), -np.sin(phase)], axis=0)

    local = rows(np.arange(ROWS))
    behind = rows(np.arange(-TAPS, 0))
    forward = np.concatenate([*split(local), *split(behind)], axis=1)
    inverse = np.concatenate(split(local.T / HALF), axis=1)
    return forward, inverse


def kernel(
    dims,
    feat,
    short,
    long,
    gout,
    fwd,
    inv,
    out,
    gs_out,
    gl_out,
    fb,
    gob,
    fwdv,
    invv,
    shortv,
    longv,
    coef,
    xf,
    kb,
    vb,
    prod,
    gfil,
    xhalo,
    yhalo,
    raw,
    packf,
    packb,
    qn,
    hs,
    xs,
    ys,
    rs,
    spec,
    filt,
    gf,
    gpack,
    gedge,
    glp,
    glrecv,
    glex,
    glex2,
    glfin,
    gsp,
    gscore,
    gsex,
    gsex2,
    gsfin,
    ld_sem,
    halo_s,
    x_r,
    y_r,
    g_r,
    gl_s,
    gl_r,
    gs_s,
    gs_r,
):
    n_seq, n_ch, n_y, n_z, lanes = dims
    tokens = ROWS * n_seq
    gs_scale = 1.0 / math.sqrt(tokens)
    gl_scale = 1.0 / math.sqrt(tokens * (lanes * n_ch // GROUPS))
    tiles = lanes // 128
    chunks = lanes // 256
    halves = tiles // 4
    s = lax.axis_index("seq")
    ch = lax.axis_index("ch")
    core = lax.rem(s, 2)
    z = lax.rem(s // 2, n_z)
    y = s // (2 * n_z)

    def at(yy, zz, cc):
        return (yy * n_z + zz) * 2 + cc

    ahead = {"seq": lax.rem(s + 1, n_seq)}
    behind = {"seq": lax.rem(s + n_seq - 1, n_seq)}
    sibling = {"seq": at(y, z, 1 - core)}

    def far_first(n):
        return sorted(range(1, n), key=lambda d: -min(d, n - d))

    ys_peers = [{"seq": at(lax.rem(y + d, n_y), z, core)} for d in far_first(n_y)]
    zs_peers = [{"seq": at(y, lax.rem(z + d, n_z), core)} for d in far_first(n_z)]
    n_own = 2 * n_ch
    own = ch * 2 + core
    xc_peers = []
    for d in range(1, n_own):
        o = lax.rem(own + d, n_own)
        xc_peers.append(({"seq": at(y, z, lax.rem(o, 2)), "ch": o // 2}, o))

    barrier = pltpu.get_barrier_semaphore()
    greet = [ahead, behind] + ys_peers + zs_peers + [p for p, _ in xc_peers]
    for p in greet:
        pl.semaphore_signal(barrier, inc=1, device_id=p, device_id_type=MESH)

    def load(src, dst, i):
        c = pltpu.make_async_copy(src, dst, ld_sem.at[i])
        c.start()
        return c

    def all_of(ref, sem):
        pltpu.make_async_copy(ref, ref, sem).wait()

    c_short = load(short, shortv, 0)
    for l in range(tiles):
        load(feat.at[:, :, l * 128 : (l + 1) * 128], fb.at[l], 1)
    for l in range(tiles):
        load(gout.at[:, l * 128 : (l + 1) * 128], gob.at[l], 2)
    c_long = load(long, longv, 3)
    c_fwd = load(fwd, fwdv, 4)
    c_inv = load(inv, invv, 5)

    def remote(src, dst, ssem, rsem, peer):
        pltpu.make_async_remote_copy(
            src_ref=src, dst_ref=dst, send_sem=ssem, recv_sem=rsem, device_id=peer, device_id_type=MESH
        ).start()

    c_short.wait()
    for i in range(3):
        taps = shortv[i].astype(F32)
        for l in range(tiles):
            coef[l, i, 0:SHORT, :] = taps[:, l * 128 : (l + 1) * 128]
    all_of(fb, ld_sem.at[1])

    def tap(l, i):
        return [coef[l, i, j : j + 1, :] for j in range(SHORT)]

    def fir(ref, l, i, c, first):
        total = c[0] * ref[l, i, first : first + 16, :]
        for j in range(1, SHORT):
            total = total + c[j] * ref[l, i, first - j : first - j + 16, :]
        return total.astype(BF)

    def widen(l, i, lo, hi):
        for r in range(lo, hi, 16):
            xf[l, i, 8 + r : 24 + r, :] = fb[l, i, r : r + 16, :].astype(F32)

    def tile(l):
        return pl.ds(pl.multiple_of(l * 128, 128), 128)

    def lane(l):
        return pl.ds(pl.multiple_of(lax.rem(l, 2) * 128, 128), 128)

    def product_rows(l, lo, hi):
        ck, cv = tap(l, 1), tap(l, 2)
        for r in range(lo, hi, 16):
            k = fir(xf, l, 1, ck, 8 + r)
            v = fir(xf, l, 2, cv, 8 + r)
            kb[l, r : r + 16, :] = k
            vb[l, r : r + 16, :] = v
            prod[l // 2, r : r + 16, lane(l)] = (k.astype(F32) * v.astype(F32)).astype(BF)

    def grad_rows(l, lo, hi):
        cq = tap(l, 0)
        for r in range(lo, hi, 16):
            q = fir(xf, l, 0, cq, 8 + r)
            gfil[l // 2, r : r + 16, lane(l)] = (
                q.astype(F32) * gob[l, r : r + 16, :].astype(F32)
            ).astype(BF)

    def tail(l, _):
        widen(l, 0, ROWS - 16, ROWS)
        widen(l, 1, 112, ROWS)
        widen(l, 2, 112, ROWS)
        product_rows(l, 128, ROWS)
        return 0

    def tails():
        lax.fori_loop(0, tiles, tail, 0)

    raw_s, pack_s, x_s, y_s, g_s, raw_r, pack_r = (halo_s.at[k] for k in range(7))

    def six(l, i):
        return slice((3 * l + i) * EDGE, (3 * l + i + 1) * EDGE)

    def packs():
        for l in range(tiles):
            for i in range(3):
                packf[six(l, i), :] = xf[l, i, 8 + ROWS - EDGE : 8 + ROWS, :]
        packb[0] = packf[...].astype(BF)

    def send_first():
        pl.semaphore_wait(barrier, len(greet))
        remote(packb.at[0], packb.at[1], pack_s, pack_r, ahead)
        remote(feat.at[0, 0:16, :], raw.at[0], raw_s, raw_r, behind)
        remote(gout.at[0:16, :], raw.at[1], raw_s, raw_r, behind)
        for q in range(chunks):
            remote(prod.at[q, ROWS - TAPS :, :], xhalo.at[q], x_s, x_r.at[q], ahead)

    def head(l, _):
        widen(l, 0, 0, 128)
        grad_rows(l, 16, 128)
        return 0

    def heads(q):
        lax.fori_loop(2 * q, 2 * q + 2, head, 0)

    def send_head(q):
        remote(gfil.at[q, 16:TAPS, :], yhalo.at[q, 16:TAPS, :], y_s, y_r.at[q], behind)

    def rest(l, _):
        widen(l, 0, 128, ROWS)
        grad_rows(l, 128, ROWS)
        widen(l, 1, 0, 112)
        widen(l, 2, 0, 112)
        product_rows(l, 16, 128)
        return 0

    def rests():
        lax.fori_loop(0, tiles, rest, 0)

    nt = (((1,), (1,)), ((), ()))

    def spectrum():
        hs[...] = lax.dot_general(fwdv[:, 0:TAPS], longv[...], nt, preferred_element_type=F32) + lax.dot_general(
        fwdv[:, ROWS : ROWS + TAPS], longv[...], nt, preferred_element_type=F32
    )

    not_first = jnp.where(s > 0, 1.0, 0.0).astype(F32)
    not_last = jnp.where(s < n_seq - 1, 1.0, 0.0).astype(F32)
    def unpack():
        packf[...] = packb[1].astype(F32) * not_first

    def edges(l):
        cols = slice(l * 128, (l + 1) * 128)
        for i in range(3):
            xf[l, i, 8 - EDGE : 8, :] = packf[six(l, i), :]
        qn[l, 0, 0:8, :] = xf[l, 0, ROWS : ROWS + 8, :]
        qn[l, 0, 8:24, :] = raw[0, :, cols].astype(F32)
        product_rows(l, 0, 16)
        grad_rows(l, 0, 16)
        qq = fir(qn, l, 0, tap(l, 0), 8)
        yhalo[l // 2, 0:16, (l % 2) * 128 : (l % 2) * 128 + 128] = (
            qq.astype(F32) * raw[1, :, cols].astype(F32)
        ).astype(BF)

    def dot(a, b):
        return jnp.dot(a, b, preferred_element_type=F32)

    def local(q):
        p = prod[q]
        xs[q] = dot(fwdv[:, 0:ROWS], p) + dot(fwdv[:, ROWS : 2 * ROWS], p)
        g = gfil[q]
        ys[q] = dot(fwdv[:, 0:ROWS], g) + dot(fwdv[:, ROWS : 2 * ROWS], g)


    def far(h):
        return dot(fwdv[:, 2 * ROWS : 2 * ROWS + TAPS], h) + dot(fwdv[:, 2 * ROWS + TAPS :], h)

    def wait_x(q):
        all_of(xhalo.at[q], x_r.at[q])

    def wait_y(q):
        all_of(yhalo.at[q, 16:TAPS, :], y_r.at[q])

    def add_x(q):
        wait_x(q)
        xs[q] = xs[q] + not_first * far(xhalo[q])

    def add_y(q):
        wait_y(q)
        ys[q] = ys[q] - not_last * far(yhalo[q])

    def corr(q, first):
        def block(b, _):
            re = pl.ds(pl.multiple_of(b * 16, 16), 16)
            im = pl.ds(pl.multiple_of(b * 16 + HALF, 16), 16)
            xr, xi, yr, yi = xs[q, re, :], xs[q, im, :], ys[q, re, :], ys[q, im, :]
            rr = xr * yr + xi * yi
            ri = xr * yi - xi * yr
            if not first:
                rr = rr + rs[re, :]
                ri = ri + rs[im, :]
            rs[re, :] = rr
            rs[im, :] = ri
            return 0

        lax.fori_loop(0, HALF // 16, block, 0)

    def hilo(value):
        high = value.astype(BF)
        return high, (value - high.astype(F32)).astype(BF)

    own_rows = TAPS // n_own

    def piece(o):
        return pl.ds(pl.multiple_of(o * own_rows, own_rows), own_rows)

    def lags():
        rh, rl = hilo(rs[...])
        glp[...] = (
            dot(invv[0:TAPS, 0:N], rh) + dot(invv[0:TAPS, N:], rh) + dot(invv[0:TAPS, 0:N], rl)
        ).astype(BF)

    rings = ((ys_peers, zs_peers), (zs_peers, ys_peers))
    places = ((y, z), (z, y))

    def spread(ref, place, value, ssem, rsem, peers):
        ref[place] = value
        for p in peers:
            remote(ref.at[place], ref.at[place], ssem, rsem, p)

    def gathered(ref, sem, count):
        all_of(ref.at[0 : count - 1], sem)
        total = ref[0].astype(F32)
        for d in range(1, count):
            total = total + ref[d].astype(F32)
        return total

    counts = ((n_y, n_z), (n_z, n_y))

    def gl_zero():
        glrecv[own] = glp[piece(own), :]
        for p, o in xc_peers:
            remote(glp.at[piece(o), :], glrecv.at[own], gl_s.at[0], gl_r.at[0], p)

    def gl_one():
        total = gathered(glrecv, gl_r.at[0], n_own)
        for k in range(2):
            part = total[:, k * 128 : (k + 1) * 128].astype(BF)
            spread(glex.at[k], places[k][0], part, gl_s.at[1 + k], gl_r.at[1 + k], rings[k][0])

    def gl_two(k):
        part = gathered(glex.at[k], gl_r.at[1 + k], counts[k][0]).astype(BF)
        spread(glex2.at[k], places[k][1], part, gl_s.at[3 + k], gl_r.at[3 + k], rings[k][1])

    def gl_three():
        for k in range(2):
            total = gathered(glex2.at[k], gl_r.at[3 + k], counts[k][1]) * gl_scale
            glfin[piece(own), k * 128 : (k + 1) * 128] = total.astype(BF)
        for p, _ in xc_peers:
            remote(glfin.at[piece(own), :], glfin.at[piece(own), :], gl_s.at[5], gl_r.at[5], p)

    def gl_four():
        all_of(glfin.at[0 : TAPS - own_rows], gl_r.at[5])
        gl_out[...] = glfin[...].astype(F32).T

    def gs_zero(h):
        theirs = pl.ds(4 * h + 2 * (1 - core), 2)
        remote(gsp.at[theirs], gscore.at[h], gs_s.at[h, 0], gs_r.at[h, 0], sibling)

    def part_rows(h, k):
        cut = 32 if h % 2 == 0 else 16
        return slice(0, cut) if k == 0 else slice(cut, 48)

    def gs_one(h):
        all_of(gscore.at[h], gs_r.at[h, 0])
        total = gsp[pl.ds(4 * h + 2 * core, 2)] + gscore[h]
        total = total.reshape(48, 128)
        for k in range(2):
            rows = part_rows(h, k)
            ref = gsex.at[h, :, rows, :]
            spread(ref, places[k][0], total[rows].astype(BF), gs_s.at[h, 1 + k], gs_r.at[h, 1 + k], rings[k][0])

    def gs_two(h):
        for k in range(2):
            rows = part_rows(h, k)
            part = gathered(gsex.at[h, :, rows, :], gs_r.at[h, 1 + k], counts[k][0]).astype(BF)
            ref = gsex2.at[h, :, rows, :]
            spread(ref, places[k][1], part, gs_s.at[h, 3 + k], gs_r.at[h, 3 + k], rings[k][1])

    def gs_three(h):
        parts = []
        for k in range(2):
            ref = gsex2.at[h, :, part_rows(h, k), :]
            parts.append(gathered(ref, gs_r.at[h, 3 + k], counts[k][1]))
        total = jnp.concatenate(parts, axis=0) * gs_scale
        here = pl.ds(4 * h + 2 * core, 2)
        gsfin[here] = total.reshape(2, 24, 128)
        remote(gsfin.at[here], gsfin.at[here], gs_s.at[h, 5], gs_r.at[h, 5], sibling)

    def gs_four(h):
        all_of(gscore.at[h], gs_r.at[h, 5])
        for l in range(4 * h, 4 * h + 4):
            for i in range(3):
                gs_out[i, :, l * 128 : (l + 1) * 128] = gsfin[l, 8 * i : 8 * i + SHORT, :]

    def spectra(q):
        def block(b, _):
            re = pl.ds(pl.multiple_of(b * 16, 16), 16)
            im = pl.ds(pl.multiple_of(b * 16 + HALF, 16), 16)
            hr, hi = hs[re, :], hs[im, :]
            xr, xi = xs[q, re, :], xs[q, im, :]
            yr, yi = ys[q, re, :], ys[q, im, :]
            parts = (
                (re, 0, xr * hr - xi * hi),
                (im, 0, xr * hi + xi * hr),
                (re, 256, yr * hr + yi * hi),
                (im, 256, yi * hr - yr * hi),
            )
            for rows, c, value in parts:
                spec[rows, c : c + 256] = value.astype(BF)
            return 0

        lax.fori_loop(0, HALF // 16, block, 0)

    def inverse():
        filt[...] = dot(invv[:, 0:N], spec[...])

    def featured_grad(l, h):
        for r in range(0, ROWS, 16):
            rows = slice(r, r + 16)
            fa = filt[rows, h * 128 : h * 128 + 128]
            fg = filt[rows, 256 + h * 128 : 256 + h * 128 + 128]
            g0 = (gob[l, rows, :].astype(F32) * fa).astype(BF)
            g1 = (fg * vb[l, rows, :].astype(F32)).astype(BF)
            g2 = (fg * kb[l, rows, :].astype(F32)).astype(BF)
            for i, g in enumerate((g0, g1, g2)):
                gf[l, i, rows, :] = g.astype(F32)

    def short_grad(l):
        for i in range(3):
            acc = [jnp.zeros((8, 128), F32) for _ in range(SHORT)]
            for r in range(0, ROWS, 8):
                g = gf[l, i, r : r + 8, :]
                for j in range(SHORT):
                    acc[j] = acc[j] + g * xf[l, i, 8 + r - j : 16 + r - j, :]
            rows = [jnp.sum(a, axis=0, keepdims=True) for a in acc]
            rows.append(jnp.zeros((1, 128), F32))
            gsp[l, 8 * i : 8 * i + 8, :] = jnp.concatenate(rows, axis=0)

    def fgrads(q):
        for h in range(2):
            featured_grad(2 * q + h, h)

    def send_grad(q):
        for h in range(2):
            for i in range(3):
                gpack[six(h, i), :] = gf[2 * q + h, i, 0:EDGE, :]
        gedge[0, q] = gpack[...].astype(BF)
        remote(gedge.at[0, q], gedge.at[1, q], g_s, g_r.at[q], behind)

    def sgrads(q):
        def sg(l, _):
            short_grad(l)
            return 0

        lax.fori_loop(2 * q, 2 * q + 2, sg, 0)

    def wait_grad(q):
        all_of(gedge.at[1, q], g_r.at[q])

    def conv(q):
        wait_grad(q)
        gpack[...] = gedge[1, q].astype(F32) * not_last
        for h in range(2):
            for i in range(3):
                gf[2 * q + h, i, ROWS : ROWS + EDGE, :] = gpack[six(h, i), :]

        def one(l, _):
            for i in range(3):
                c = tap(l, i)
                for r in range(0, ROWS, 16):
                    total = c[0] * gf[l, i, r : r + 16, :]
                    for j in range(1, SHORT):
                        total = total + c[j] * gf[l, i, r + j : r + j + 16, :]
                    out[i, r : r + 16, tile(l)] = total.astype(BF)
            return 0

        lax.fori_loop(2 * q, 2 * q + 2, one, 0)

    gpack[6 * EDGE :, :] = jnp.zeros((48 - 6 * EDGE, 128), F32)
    tails()
    packs()
    send_first()
    all_of(gob, ld_sem.at[2])
    order = list(range(chunks // 2, chunks)) + list(range(chunks // 2))
    for q in order:
        heads(q)
        send_head(q)
    rests()
    c_long.wait()
    c_fwd.wait()
    spectrum()
    all_of(packb.at[1], pack_r)
    all_of(raw, raw_r)
    unpack()
    for l in range(tiles):
        edges(l)
    for q in range(chunks):
        local(q)
    for q in range(chunks // 2):
        add_x(q)
        corr(q, q == 0)
        add_y(q + chunks // 2)
        corr(q + chunks // 2, False)
    c_inv.wait()
    lags()
    gl_zero()

    def chunk(q):
        if q < chunks // 2:
            add_y(q)
        else:
            add_x(q)
        spectra(q)
        inverse()
        fgrads(q)
        send_grad(q)
        sgrads(q)

    chunk(0)
    chunk(1)
    gs_zero(0)
    chunk(2)
    gl_one()
    gs_one(0)
    chunk(3)
    gs_zero(1)
    conv(0)
    gs_one(1)
    conv(1)
    conv(2)
    gl_two(0)
    gl_two(1)
    gs_two(0)
    conv(3)
    gs_two(1)
    gl_three()
    gs_three(0)
    gs_three(1)
    gs_four(0)
    gl_four()
    gs_four(1)

    all_of(raw, raw_s)
    all_of(packb.at[0], pack_s)
    all_of(xhalo, x_s)
    all_of(yhalo.at[:, 16:TAPS, :], y_s)
    all_of(gedge.at[0], g_s)
    all_of(glrecv.at[0 : n_own - 1], gl_s.at[0])
    for k in range(2):
        all_of(glex.at[k, 0 : counts[k][0] - 1], gl_s.at[1 + k])
        all_of(glex2.at[k, 0 : counts[k][1] - 1], gl_s.at[3 + k])
    all_of(glrecv.at[0 : n_own - 1], gl_s.at[5])
    for h in range(halves):
        all_of(gscore.at[h], gs_s.at[h, 0])
        for k in range(2):
            rows = part_rows(h, k)
            all_of(gsex.at[h, 0 : counts[k][0] - 1, rows, :], gs_s.at[h, 1 + k])
            all_of(gsex2.at[h, 0 : counts[k][1] - 1, rows, :], gs_s.at[h, 3 + k])
        all_of(gscore.at[h], gs_s.at[h, 5])


def emit(*refs):
    sem = refs[-1]
    copies = [pltpu.make_async_copy(refs[i], refs[3 + i], sem.at[i]) for i in range(3)]
    for c in copies:
        c.start()
    for c in copies:
        c.wait()


def solution(mesh):
    n_seq, n_ch = mesh.shape["seq"], mesh.shape["ch"]
    n_z = math.isqrt(n_seq // 2)
    n_y = n_seq // (2 * n_z)
    forward, inverse = transforms()

    def body(features, short_filter, long_filter, grad_out):
        lanes = features.shape[2]
        tiles, chunks, halves = lanes // 128, lanes // 256, lanes // 512
        n_own = 2 * n_ch
        own_rows = TAPS // n_own
        most = max(n_y, n_z)
        any_spec = pl.BlockSpec(memory_space=pltpu.HBM)
        vmem = pl.BlockSpec(memory_space=pltpu.VMEM)
        V = pltpu.VMEM
        D = pltpu.SemaphoreType.DMA
        results = pl.pallas_call(
            functools.partial(kernel, (n_seq, n_ch, n_y, n_z, lanes)),
            out_shape=(
                V((3, ROWS, lanes), BF),
                V((3, SHORT, lanes), F32),
                V((GROUPS, TAPS), F32),
            ),
            in_specs=[any_spec] * 6,
            out_specs=(vmem, vmem, vmem),
            scratch_shapes=[
                V((tiles, 3, ROWS, 128), BF),
                V((tiles, ROWS, 128), BF),
                V((N, 2 * N), BF),
                V((ROWS, 2 * N), BF),
                V((3, SHORT, lanes), BF),
                V((GROUPS, TAPS), BF),
                V((tiles, 3, 8, 128), F32),
                V((tiles, 3, ROWS + 8, 128), F32),
                V((tiles, ROWS, 128), BF),
                V((tiles, ROWS, 128), BF),
                V((chunks, ROWS, 256), BF),
                V((chunks, ROWS, 256), BF),
                V((chunks, TAPS, 256), BF),
                V((chunks, TAPS, 256), BF),
                V((2, 16, lanes), BF),
                V((tiles * 3 * EDGE, 128), F32),
                V((2, tiles * 3 * EDGE, 128), BF),
                V((tiles, 1, 24, 128), F32),
                V((N, 256), F32),
                V((chunks, N, 256), F32),
                V((chunks, N, 256), F32),
                V((N, 256), F32),
                V((N, 512), BF),
                V((ROWS, 512), F32),
                V((tiles, 3, ROWS + 8, 128), F32),
                V((48, 128), F32),
                V((2, chunks, 48, 128), BF),
                V((TAPS, 256), BF),
                V((n_own, own_rows, 256), BF),
                V((2, most, own_rows, 128), BF),
                V((2, most, own_rows, 128), BF),
                V((TAPS, 256), BF),
                V((tiles, 24, 128), F32),
                V((halves, 2, 24, 128), F32),
                V((halves, most, 48, 128), BF),
                V((halves, most, 48, 128), BF),
                V((tiles, 24, 128), F32),
                D((6,)),
                D((7,)),
                D((chunks,)),
                D((chunks,)),
                D((chunks,)),
                D((6,)),
                D((6,)),
                D((halves, 6)),
                D((halves, 6)),
            ],
            compiler_params=pltpu.CompilerParams(
                collective_id=0, has_side_effects=True, vmem_limit_bytes=40 * 2**20
            ),
            name="hyena_backward",
        )(
            *(
                pltpu.with_memory_space_constraint(a, pltpu.HBM)
                for a in (features, short_filter, long_filter, grad_out, jnp.asarray(forward), jnp.asarray(inverse))
            )
        )
        grad_features, grad_short, grad_long = pl.pallas_call(
            emit,
            out_shape=tuple(jax.ShapeDtypeStruct(r.shape, r.dtype) for r in results),
            in_specs=[vmem] * 3,
            out_specs=(pl.BlockSpec(memory_space=pl.ANY),) * 3,
            scratch_shapes=[D((3,))],
            name="emit",
        )(*(pltpu.with_memory_space_constraint(r, pltpu.VMEM) for r in results))
        return grad_features, grad_short, grad_long

    return jax.shard_map(
        body,
        mesh=mesh,
        in_specs=(P(None, "seq", "ch"), P(None, None, "ch"), P(), P("seq", "ch")),
        out_specs=(P(None, "seq", "ch"), P(None, None, "ch"), P()),
        check_vma=False,
    )
```

```python
import functools
import math

import jax
import jax.numpy as jnp
import ml_dtypes
import numpy as np
from jax import lax
from jax.experimental import pallas as pl
from jax.experimental.pallas import tpu as pltpu
from jax.sharding import PartitionSpec as P

MESH = pl.DeviceIdType.MESH
BF = jnp.bfloat16
F32 = jnp.float32
ROWS = 256
TAPS = 128
SHORT = 7
EDGE = SHORT - 1
LATE = 112
GROUPS = 256
N = ROWS + TAPS
HALF = N // 2


def split(matrix):
    high = matrix.astype(ml_dtypes.bfloat16)
    low = (matrix - high.astype(np.float64)).astype(ml_dtypes.bfloat16)
    return high, low


def transforms():
    angle = 2 * np.pi * (np.arange(HALF) + 0.5) / N

    def rows(tokens):
        phase = np.outer(angle, tokens)
        return np.concatenate([np.cos(phase), -np.sin(phase)], axis=0)

    local = rows(np.arange(ROWS))
    behind = rows(np.arange(-TAPS, 0))
    edge = np.concatenate([part[:, :16] for part in split(local)], axis=1)
    blank = np.zeros((N, 96), ml_dtypes.bfloat16)
    forward = np.concatenate([*split(local), *split(behind), edge, blank], axis=1)
    inverse = np.concatenate(split(local.T / HALF), axis=1)
    return forward, inverse


def kernel(
    dims,
    feat,
    short,
    long,
    gout,
    fwd,
    inv,
    out,
    gs_out,
    gl_out,
    fb,
    gob,
    fwdv,
    invv,
    shortv,
    longv,
    coef,
    xf,
    kb,
    vb,
    prod,
    gfil,
    ends,
    xhalo,
    yhalo,
    raw,
    packf,
    packb,
    qn,
    hs,
    xs,
    ys,
    rs,
    spec,
    filt,
    gf,
    gpack,
    gedge,
    glp,
    glrecv,
    glex,
    glex2,
    glfin,
    gsp,
    gscore,
    gsex,
    gsex2,
    gsfin,
    ld_sem,
    halo_s,
    halo_r,
    x_r,
    y_r,
    g_r,
    gl_s,
    gl_r,
    gs_s,
    gs_r,
):
    n_seq, n_ch, n_y, n_z, lanes = dims
    tokens = ROWS * n_seq
    gs_scale = 1.0 / math.sqrt(tokens)
    gl_scale = 1.0 / math.sqrt(tokens * (lanes * n_ch // GROUPS))
    tiles = lanes // 128
    chunks = lanes // 256
    halves = tiles // 4
    s = lax.axis_index("seq")
    ch = lax.axis_index("ch")
    core = lax.rem(s, 2)
    z = lax.rem(s // 2, n_z)
    y = s // (2 * n_z)

    def at(yy, zz, cc):
        return (yy * n_z + zz) * 2 + cc

    ahead = {"seq": lax.rem(s + 1, n_seq)}
    behind = {"seq": lax.rem(s + n_seq - 1, n_seq)}
    sibling = {"seq": at(y, z, 1 - core)}

    def far_first(n):
        return sorted(range(1, n), key=lambda d: -min(d, n - d))

    ys_peers = [{"seq": at(lax.rem(y + d, n_y), z, core)} for d in far_first(n_y)]
    zs_peers = [{"seq": at(y, lax.rem(z + d, n_z), core)} for d in far_first(n_z)]
    n_own = 2 * n_ch
    own = ch * 2 + core
    xc_peers = []
    for d in range(1, n_own):
        o = lax.rem(own + d, n_own)
        xc_peers.append(({"seq": at(y, z, lax.rem(o, 2)), "ch": o // 2}, o))

    barrier = pltpu.get_barrier_semaphore()
    greet = [ahead, behind] + ys_peers + zs_peers + [p for p, _ in xc_peers]
    for p in greet:
        pl.semaphore_signal(barrier, inc=1, device_id=p, device_id_type=MESH)

    def load(src, dst, i):
        c = pltpu.make_async_copy(src, dst, ld_sem.at[i])
        c.start()
        return c

    def all_of(ref, sem):
        pltpu.make_async_copy(ref, ref, sem).wait()

    c_short = load(short, shortv, 0)
    for l in range(tiles):
        load(feat.at[:, LATE:, l * 128 : (l + 1) * 128], fb.at[l, :, LATE:, :], 1)
    for l in range(tiles):
        load(gout.at[:, l * 128 : (l + 1) * 128], gob.at[l], 2)
    for l in range(tiles):
        load(feat.at[:, :LATE, l * 128 : (l + 1) * 128], fb.at[l, :, :LATE, :], 6)
    c_long = load(long, longv, 3)
    c_fwd = load(fwd, fwdv, 4)
    c_inv = load(inv, invv, 5)

    def remote(src, dst, ssem, rsem, peer):
        pltpu.make_async_remote_copy(
            src_ref=src, dst_ref=dst, send_sem=ssem, recv_sem=rsem, device_id=peer, device_id_type=MESH
        ).start()

    c_short.wait()
    for i in range(3):
        taps = shortv[i].astype(F32)
        for l in range(tiles):
            coef[l, i, 0:SHORT, :] = taps[:, l * 128 : (l + 1) * 128]

    def tap(l, i):
        return [coef[l, i, j : j + 1, :] for j in range(SHORT)]

    def fir(ref, l, i, c, first):
        total = c[0] * ref[l, i, first : first + 16, :]
        for j in range(1, SHORT):
            total = total + c[j] * ref[l, i, first - j : first - j + 16, :]
        return total.astype(BF)

    def widen(l, i, lo, hi):
        for r in range(lo, hi, 16):
            xf[l, i, 8 + r : 24 + r, :] = fb[l, i, r : r + 16, :].astype(F32)

    def tile(l):
        return pl.ds(pl.multiple_of(l * 128, 128), 128)

    def lane(l):
        if isinstance(l, int):
            return slice((l % 2) * 128, (l % 2) * 128 + 128)
        return pl.ds(pl.multiple_of(lax.rem(l, 2) * 128, 128), 128)

    def product_rows(l, lo, hi, near=False):
        ck, cv = tap(l, 1), tap(l, 2)
        for r in range(lo, hi, 16):
            k = fir(xf, l, 1, ck, 8 + r)
            v = fir(xf, l, 2, cv, 8 + r)
            kb[l, r : r + 16, :] = k
            vb[l, r : r + 16, :] = v
            p = (k.astype(F32) * v.astype(F32)).astype(BF)
            if near:
                ends[l // 2, 0:16, lane(l)] = p
                ends[l // 2, 16:32, lane(l)] = p
            else:
                prod[l // 2, r : r + 16, lane(l)] = p

    def grad_rows(l, lo, hi, near=False):
        cq = tap(l, 0)
        for r in range(lo, hi, 16):
            q = fir(xf, l, 0, cq, 8 + r)
            g = (q.astype(F32) * gob[l, r : r + 16, :].astype(F32)).astype(BF)
            if near:
                c = (l % 2) * 128 + 256
                ends[l // 2, 0:16, c : c + 128] = g
                ends[l // 2, 16:32, c : c + 128] = g
            else:
                gfil[l // 2, r : r + 16, lane(l)] = g

    def lasts():
        for l in range(tiles):
            for i in range(3):
                widen(l, i, ROWS - 16, ROWS)

    def tail(l, _):
        widen(l, 1, LATE, ROWS - 16)
        widen(l, 2, LATE, ROWS - 16)
        product_rows(l, 128, ROWS)
        return 0

    def tails(q):
        lax.fori_loop(2 * q, 2 * q + 2, tail, 0)

    raw_s = x_s = y_s = g_s = halo_s.at[0]
    pack_s = halo_s.at[1]
    raw_r, pack_r = halo_r.at[0], halo_r.at[1]

    def six(l, i):
        return slice((3 * l + i) * EDGE, (3 * l + i + 1) * EDGE)

    def packs():
        for l in range(tiles):
            for i in range(3):
                packf[six(l, i), :] = xf[l, i, 8 + ROWS - EDGE : 8 + ROWS, :]
        packb[0] = packf[...].astype(BF)

    def send_first():
        pl.semaphore_wait(barrier, len(greet))
        remote(packb.at[0], packb.at[1], pack_s, pack_r, ahead)
        remote(feat.at[0, 0:16, :], raw.at[0], raw_s, raw_r, behind)
        remote(gout.at[0:16, :], raw.at[1], raw_s, raw_r, behind)

    def send_tail(q):
        remote(prod.at[q, ROWS - TAPS :, :], xhalo.at[q], x_s, x_r.at[q], ahead)

    def head(l, _):
        widen(l, 0, 0, 128)
        grad_rows(l, 16, 128)
        return 0

    def heads(q):
        lax.fori_loop(2 * q, 2 * q + 2, head, 0)

    def send_head(q):
        remote(gfil.at[q, 16:TAPS, :], yhalo.at[q, 16:TAPS, :], y_s, y_r.at[q], behind)

    def rest(l):
        widen(l, 0, 128, ROWS - 16)
        grad_rows(l, 128, ROWS)
        widen(l, 1, 0, LATE)
        widen(l, 2, 0, LATE)
        product_rows(l, 16, 128)

    nt = (((1,), (1,)), ((), ()))

    def spectrum():
        hs[...] = lax.dot_general(fwdv[:, 0:TAPS], longv[...], nt, preferred_element_type=F32) + lax.dot_general(
        fwdv[:, ROWS : ROWS + TAPS], longv[...], nt, preferred_element_type=F32
    )

    not_first = jnp.where(s > 0, 1.0, 0.0).astype(F32)
    not_last = jnp.where(s < n_seq - 1, 1.0, 0.0).astype(F32)
    def unpack():
        packf[...] = packb[1].astype(F32) * not_first

    def edges(l):
        cols = slice(l * 128, (l + 1) * 128)
        for i in range(3):
            xf[l, i, 8 - EDGE : 8, :] = packf[six(l, i), :]
        qn[l, 0, 0:8, :] = xf[l, 0, ROWS : ROWS + 8, :]
        qn[l, 0, 8:24, :] = raw[0, :, cols].astype(F32)
        product_rows(l, 0, 16, near=True)
        grad_rows(l, 0, 16, near=True)
        qq = fir(qn, l, 0, tap(l, 0), 8)
        yhalo[l // 2, 0:16, (l % 2) * 128 : (l % 2) * 128 + 128] = (
            qq.astype(F32) * raw[1, :, cols].astype(F32)
        ).astype(BF)

    def dot(a, b):
        return jnp.dot(a, b, preferred_element_type=F32)

    def local(q):
        p = prod[q]
        xs[q] = dot(fwdv[:, 0:ROWS], p) + dot(fwdv[:, ROWS : 2 * ROWS], p)
        g = gfil[q]
        ys[q] = dot(fwdv[:, 0:ROWS], g) + dot(fwdv[:, ROWS : 2 * ROWS], g)


    def far(h):
        return dot(fwdv[:, 2 * ROWS : 2 * ROWS + TAPS], h) + dot(fwdv[:, 2 * ROWS + TAPS : 2 * N], h)

    def wait_x(q):
        all_of(xhalo.at[q], x_r.at[q])

    def wait_y(q):
        all_of(yhalo.at[q, 16:TAPS, :], y_r.at[q])

    def add_x(q):
        wait_x(q)
        xs[q] = xs[q] + not_first * far(xhalo[q])

    def add_y(q):
        wait_y(q)
        ys[q] = ys[q] - not_last * far(yhalo[q])

    def both(halo, sign, near):
        h = (halo.astype(F32) * sign).astype(BF)
        return dot(fwdv[:, 2 * ROWS :], jnp.concatenate([h, h, near], axis=0))

    def add_ends(q):
        if q < chunks // 2:
            wait_x(q)
            xs[q] = xs[q] + both(xhalo[q], not_first, ends[q, :, 0:256])
            ys[q] = ys[q] + dot(fwdv[:, 2 * N :], ends[q, :, 256:512])
        else:
            wait_y(q)
            ys[q] = ys[q] + both(yhalo[q], -not_last, ends[q, :, 256:512])
            xs[q] = xs[q] + dot(fwdv[:, 2 * N :], ends[q, :, 0:256])

    def corr(q, first):
        def block(b, _):
            re = pl.ds(pl.multiple_of(b * 16, 16), 16)
            im = pl.ds(pl.multiple_of(b * 16 + HALF, 16), 16)
            xr, xi, yr, yi = xs[q, re, :], xs[q, im, :], ys[q, re, :], ys[q, im, :]
            rr = xr * yr + xi * yi
            ri = xr * yi - xi * yr
            if not first:
                rr = rr + rs[re, :]
                ri = ri + rs[im, :]
            rs[re, :] = rr
            rs[im, :] = ri
            return 0

        lax.fori_loop(0, HALF // 16, block, 0, unroll=True)

    def hilo(value):
        high = value.astype(BF)
        return high, (value - high.astype(F32)).astype(BF)

    own_rows = TAPS // n_own

    def piece(o):
        return pl.ds(pl.multiple_of(o * own_rows, own_rows), own_rows)

    def lags():
        rh, rl = hilo(rs[...])
        glp[...] = (
            dot(invv[0:TAPS, 0:N], rh) + dot(invv[0:TAPS, N:], rh) + dot(invv[0:TAPS, 0:N], rl)
        ).astype(BF)

    rings = ((ys_peers, zs_peers), (zs_peers, ys_peers))
    places = ((y, z), (z, y))

    def spread(ref, place, value, ssem, rsem, peers):
        ref[place] = value
        for p in peers:
            remote(ref.at[place], ref.at[place], ssem, rsem, p)

    def gathered(ref, sem, count):
        all_of(ref.at[0 : count - 1], sem)
        total = ref[0].astype(F32)
        for d in range(1, count):
            total = total + ref[d].astype(F32)
        return total

    counts = ((n_y, n_z), (n_z, n_y))

    def gl_zero():
        glrecv[own] = glp[piece(own), :]
        for p, o in xc_peers:
            remote(glp.at[piece(o), :], glrecv.at[own], gl_s, gl_r.at[0], p)

    def gl_one():
        total = gathered(glrecv, gl_r.at[0], n_own)
        for k in range(2):
            part = total[:, k * 128 : (k + 1) * 128].astype(BF)
            spread(glex.at[k], places[k][0], part, gl_s, gl_r.at[1 + k], rings[k][0])

    def gl_two(k):
        part = gathered(glex.at[k], gl_r.at[1 + k], counts[k][0]).astype(BF)
        spread(glex2.at[k], places[k][1], part, gl_s, gl_r.at[3 + k], rings[k][1])

    def gl_three():
        for k in range(2):
            total = gathered(glex2.at[k], gl_r.at[3 + k], counts[k][1]) * gl_scale
            glfin[piece(own), k * 128 : (k + 1) * 128] = total.astype(BF)
        for p, _ in xc_peers:
            remote(glfin.at[piece(own), :], glfin.at[piece(own), :], gl_s, gl_r.at[5], p)

    def gl_four():
        all_of(glfin.at[0 : TAPS - own_rows], gl_r.at[5])
        gl_out[...] = glfin[...].astype(F32).T

    def gs_zero(h):
        theirs = pl.ds(4 * h + 2 * (1 - core), 2)
        remote(gsp.at[theirs], gscore.at[h], gs_s.at[h], gs_r.at[h, 0], sibling)

    def part_rows(h, k):
        cut = 32 if h % 2 == 0 else 16
        return slice(0, cut) if k == 0 else slice(cut, 48)

    def gs_one(h):
        all_of(gscore.at[h], gs_r.at[h, 0])
        total = gsp[pl.ds(4 * h + 2 * core, 2)] + gscore[h]
        total = total.reshape(48, 128)
        for k in range(2):
            rows = part_rows(h, k)
            ref = gsex.at[h, :, rows, :]
            spread(ref, places[k][0], total[rows].astype(BF), gs_s.at[h], gs_r.at[h, 1 + k], rings[k][0])

    def gs_two(h):
        for k in range(2):
            rows = part_rows(h, k)
            part = gathered(gsex.at[h, :, rows, :], gs_r.at[h, 1 + k], counts[k][0]).astype(BF)
            ref = gsex2.at[h, :, rows, :]
            spread(ref, places[k][1], part, gs_s.at[h], gs_r.at[h, 3 + k], rings[k][1])

    def gs_three(h):
        parts = []
        for k in range(2):
            ref = gsex2.at[h, :, part_rows(h, k), :]
            parts.append(gathered(ref, gs_r.at[h, 3 + k], counts[k][1]))
        total = jnp.concatenate(parts, axis=0) * gs_scale
        here = pl.ds(4 * h + 2 * core, 2)
        gsfin[here] = total.reshape(2, 24, 128)
        remote(gsfin.at[here], gsfin.at[here], gs_s.at[h], gs_r.at[h, 5], sibling)

    def gs_four(h):
        all_of(gscore.at[h], gs_r.at[h, 5])
        for l in range(4 * h, 4 * h + 4):
            for i in range(3):
                gs_out[i, :, l * 128 : (l + 1) * 128] = gsfin[l, 8 * i : 8 * i + SHORT, :]

    def spectra(q):
        def block(b, _):
            re = pl.ds(pl.multiple_of(b * 16, 16), 16)
            im = pl.ds(pl.multiple_of(b * 16 + HALF, 16), 16)
            hr, hi = hs[re, :], hs[im, :]
            xr, xi = xs[q, re, :], xs[q, im, :]
            yr, yi = ys[q, re, :], ys[q, im, :]
            parts = (
                (re, 0, xr * hr - xi * hi),
                (im, 0, xr * hi + xi * hr),
                (re, 256, yr * hr + yi * hi),
                (im, 256, yi * hr - yr * hi),
            )
            for rows, c, value in parts:
                spec[rows, c : c + 256] = value.astype(BF)
            return 0

        lax.fori_loop(0, HALF // 16, block, 0, unroll=3)

    def inverse():
        filt[...] = dot(invv[:, 0:N], spec[...])

    def featured_grad(l, h):
        for r in range(0, ROWS, 16):
            rows = slice(r, r + 16)
            fa = filt[rows, h * 128 : h * 128 + 128]
            fg = filt[rows, 256 + h * 128 : 256 + h * 128 + 128]
            g0 = (gob[l, rows, :].astype(F32) * fa).astype(BF)
            g1 = (fg * vb[l, rows, :].astype(F32)).astype(BF)
            g2 = (fg * kb[l, rows, :].astype(F32)).astype(BF)
            for i, g in enumerate((g0, g1, g2)):
                gf[l, i, rows, :] = g.astype(F32)

    def short_grad(l):
        for i in range(3):
            acc = [jnp.zeros((8, 128), F32) for _ in range(SHORT)]
            for r in range(0, ROWS, 8):
                g = gf[l, i, r : r + 8, :]
                for j in range(SHORT):
                    acc[j] = acc[j] + g * xf[l, i, 8 + r - j : 16 + r - j, :]
            rows = [jnp.sum(a, axis=0, keepdims=True) for a in acc]
            rows.append(jnp.zeros((1, 128), F32))
            gsp[l, 8 * i : 8 * i + 8, :] = jnp.concatenate(rows, axis=0)

    def fgrads(q):
        for h in range(2):
            featured_grad(2 * q + h, h)

    def send_grad(q):
        for h in range(2):
            for i in range(3):
                gpack[six(h, i), :] = gf[2 * q + h, i, 0:EDGE, :]
        gedge[0, q] = gpack[...].astype(BF)
        remote(gedge.at[0, q], gedge.at[1, q], g_s, g_r.at[q], behind)

    def sgrads(q):
        def sg(l, _):
            short_grad(l)
            return 0

        lax.fori_loop(2 * q, 2 * q + 2, sg, 0)

    def wait_grad(q):
        all_of(gedge.at[1, q], g_r.at[q])

    def conv(q):
        wait_grad(q)
        gpack[...] = gedge[1, q].astype(F32) * not_last
        for h in range(2):
            for i in range(3):
                gf[2 * q + h, i, ROWS : ROWS + EDGE, :] = gpack[six(h, i), :]

        def one(l, _):
            for i in range(3):
                c = tap(l, i)
                for r in range(0, ROWS, 16):
                    total = c[0] * gf[l, i, r : r + 16, :]
                    for j in range(1, SHORT):
                        total = total + c[j] * gf[l, i, r + j : r + j + 16, :]
                    out[i, r : r + 16, tile(l)] = total.astype(BF)
            return 0

        lax.fori_loop(2 * q, 2 * q + 2, one, 0)

    for q in range(chunks):
        prod[q, 0:16, :] = jnp.zeros((16, 256), BF)
        gfil[q, 0:16, :] = jnp.zeros((16, 256), BF)
        ends[q, 32:, :] = jnp.zeros((96, 512), BF)
    gpack[6 * EDGE :, :] = jnp.zeros((48 - 6 * EDGE, 128), F32)
    all_of(fb.at[:, :, LATE:, :], ld_sem.at[1])
    lasts()
    packs()
    first, second = list(range(chunks // 2)), list(range(chunks // 2, chunks))
    for q in first:
        tails(q)
    send_first()
    for q in first:
        send_tail(q)
    all_of(gob, ld_sem.at[2])
    all_of(fb.at[:, :, :LATE, :], ld_sem.at[6])
    for q in second:
        heads(q)
        send_head(q)
    for q in second:
        tails(q)
        send_tail(q)
    for q in first:
        heads(q)
        send_head(q)
    c_fwd.wait()
    for q in range(chunks):
        rest(2 * q)
        rest(2 * q + 1)
        local(q)
    all_of(packb.at[1], pack_r)
    all_of(raw, raw_r)
    unpack()
    for l in range(tiles):
        edges(l)
    for q in range(chunks // 2):
        add_ends(q)
        corr(q, q == 0)
        add_ends(q + chunks // 2)
        corr(q + chunks // 2, False)
    c_inv.wait()
    lags()
    gl_zero()
    c_long.wait()
    spectrum()

    def chunk(h, c):
        q = 2 * h + c
        if h < halves // 2:
            add_y(q)
        else:
            add_x(q)
        spectra(q)
        inverse()
        fgrads(q)
        send_grad(q)
        sgrads(q)

    chunk(0, 1 - core)
    gs_zero(0)
    chunk(0, core)
    gs_one(0)
    chunk(1, 1 - core)
    gs_zero(1)
    gl_one()
    chunk(1, core)
    gs_one(1)
    conv(0)
    conv(1)
    conv(2)
    conv(3)
    gs_two(0)
    gl_two(0)
    gl_two(1)
    gs_two(1)
    gl_three()
    gs_three(0)
    gs_three(1)
    gs_four(0)
    gl_four()
    gs_four(1)

    def left(sem, *refs):
        size = sum(math.prod(r.shape) * jnp.dtype(r.dtype).itemsize for r in refs)
        lines = size // 1024
        view = xs.at[0, 0:lines, :] if lines <= N else xs.at[0:2, 0 : lines // 2, :]
        assert math.prod(view.shape) * 4 == size
        all_of(view, sem)

    all_of(packb.at[0], pack_s)
    left(halo_s.at[0], raw, xhalo, yhalo.at[:, 16:TAPS, :], gedge.at[0])
    sent = [glrecv.at[0 : n_own - 1]] * 2
    for k in range(2):
        sent += [glex.at[k, 0 : counts[k][0] - 1], glex2.at[k, 0 : counts[k][1] - 1]]
    left(gl_s, *sent)
    for h in range(halves):
        sent = [gscore.at[h]] * 2
        for k in range(2):
            rows = part_rows(h, k)
            sent += [gsex.at[h, 0 : counts[k][0] - 1, rows, :], gsex2.at[h, 0 : counts[k][1] - 1, rows, :]]
        left(gs_s.at[h], *sent)


def emit(*refs):
    sem = refs[-1]
    copies = [pltpu.make_async_copy(refs[i], refs[3 + i], sem.at[i]) for i in range(3)]
    for c in copies:
        c.start()
    for c in copies:
        c.wait()


def solution(mesh):
    n_seq, n_ch = mesh.shape["seq"], mesh.shape["ch"]
    n_z = math.isqrt(n_seq // 2)
    n_y = n_seq // (2 * n_z)
    forward, inverse = transforms()

    def body(features, short_filter, long_filter, grad_out):
        lanes = features.shape[2]
        tiles, chunks, halves = lanes // 128, lanes // 256, lanes // 512
        n_own = 2 * n_ch
        own_rows = TAPS // n_own
        most = max(n_y, n_z)
        any_spec = pl.BlockSpec(memory_space=pltpu.HBM)
        vmem = pl.BlockSpec(memory_space=pltpu.VMEM)
        V = pltpu.VMEM
        D = pltpu.SemaphoreType.DMA
        results = pl.pallas_call(
            functools.partial(kernel, (n_seq, n_ch, n_y, n_z, lanes)),
            out_shape=(
                V((3, ROWS, lanes), BF),
                V((3, SHORT, lanes), F32),
                V((GROUPS, TAPS), F32),
            ),
            in_specs=[any_spec] * 6,
            out_specs=(vmem, vmem, vmem),
            scratch_shapes=[
                V((tiles, 3, ROWS, 128), BF),
                V((tiles, ROWS, 128), BF),
                V((N, 2 * N + 128), BF),
                V((ROWS, 2 * N), BF),
                V((3, SHORT, lanes), BF),
                V((GROUPS, TAPS), BF),
                V((tiles, 3, 8, 128), F32),
                V((tiles, 3, ROWS + 8, 128), F32),
                V((tiles, ROWS, 128), BF),
                V((tiles, ROWS, 128), BF),
                V((chunks, ROWS, 256), BF),
                V((chunks, ROWS, 256), BF),
                V((chunks, 128, 512), BF),
                V((chunks, TAPS, 256), BF),
                V((chunks, TAPS, 256), BF),
                V((2, 16, lanes), BF),
                V((tiles * 3 * EDGE, 128), F32),
                V((2, tiles * 3 * EDGE, 128), BF),
                V((tiles, 1, 24, 128), F32),
                V((N, 256), F32),
                V((chunks, N, 256), F32),
                V((chunks, N, 256), F32),
                V((N, 256), F32),
                V((N, 512), BF),
                V((ROWS, 512), F32),
                V((tiles, 3, ROWS + 8, 128), F32),
                V((48, 128), F32),
                V((2, chunks, 48, 128), BF),
                V((TAPS, 256), BF),
                V((n_own, own_rows, 256), BF),
                V((2, most, own_rows, 128), BF),
                V((2, most, own_rows, 128), BF),
                V((TAPS, 256), BF),
                V((tiles, 24, 128), F32),
                V((halves, 2, 24, 128), F32),
                V((halves, most, 48, 128), BF),
                V((halves, most, 48, 128), BF),
                V((tiles, 24, 128), F32),
                D((7,)),
                D((2,)),
                D((2,)),
                D((chunks,)),
                D((chunks,)),
                D((chunks,)),
                D,
                D((6,)),
                D((halves,)),
                D((halves, 6)),
            ],
            compiler_params=pltpu.CompilerParams(
                collective_id=0, has_side_effects=True, vmem_limit_bytes=40 * 2**20
            ),
            name="hyena_backward",
        )(
            *(
                pltpu.with_memory_space_constraint(a, pltpu.HBM)
                for a in (features, short_filter, long_filter, grad_out, jnp.asarray(forward), jnp.asarray(inverse))
            )
        )
        grad_features, grad_short, grad_long = pl.pallas_call(
            emit,
            out_shape=tuple(jax.ShapeDtypeStruct(r.shape, r.dtype) for r in results),
            in_specs=[vmem] * 3,
            out_specs=(pl.BlockSpec(memory_space=pl.ANY),) * 3,
            scratch_shapes=[D((3,))],
            name="emit",
        )(*(pltpu.with_memory_space_constraint(r, pltpu.VMEM) for r in results))
        return grad_features, grad_short, grad_long

    return jax.shard_map(
        body,
        mesh=mesh,
        in_specs=(P(None, "seq", "ch"), P(None, None, "ch"), P(), P("seq", "ch")),
        out_specs=(P(None, "seq", "ch"), P(None, None, "ch"), P()),
        check_vma=False,
    )
```

```python
import functools
import math

import jax
import jax.numpy as jnp
import ml_dtypes
import numpy as np
from jax import lax
from jax.experimental import pallas as pl
from jax.experimental.pallas import tpu as pltpu
from jax.sharding import PartitionSpec as P

MESH = pl.DeviceIdType.MESH
BF = jnp.bfloat16
F32 = jnp.float32
ROWS = 256
TAPS = 128
SHORT = 7
EDGE = SHORT - 1
LATE = 112
GROUPS = 256
N = ROWS + TAPS
HALF = N // 2


def split(matrix):
    high = matrix.astype(ml_dtypes.bfloat16)
    low = (matrix - high.astype(np.float64)).astype(ml_dtypes.bfloat16)
    return high, low


def transforms():
    angle = 2 * np.pi * (np.arange(HALF) + 0.5) / N

    def rows(tokens):
        phase = np.outer(angle, tokens)
        return np.concatenate([np.cos(phase), -np.sin(phase)], axis=0)

    local = rows(np.arange(ROWS))
    behind = rows(np.arange(-TAPS, 0))
    edge = np.concatenate([part[:, :16] for part in split(local)], axis=1)
    blank = np.zeros((N, 96), ml_dtypes.bfloat16)
    forward = np.concatenate([*split(local), *split(behind), edge, blank], axis=1)
    inverse = np.concatenate(split(local.T / HALF), axis=1)
    return forward, inverse


def kernel(
    dims,
    feat,
    short,
    long,
    gout,
    fwd,
    inv,
    out,
    gs_out,
    gl_out,
    fb,
    gob,
    fwdv,
    invv,
    shortv,
    longv,
    coef,
    xf,
    kb,
    vb,
    prod,
    gfil,
    ends,
    xhalo,
    yhalo,
    raw,
    packf,
    packb,
    qn,
    hs,
    xs,
    ys,
    rs,
    spec,
    filt,
    gf,
    gpack,
    gedge,
    glp,
    glrecv,
    glex,
    glex2,
    glfin,
    gsp,
    gscore,
    gsex,
    gsex2,
    gsfin,
    ld_sem,
    halo_s,
    halo_r,
    x_r,
    y_r,
    g_r,
    gl_s,
    gl_r,
    gs_s,
    gs_r,
):
    n_seq, n_ch, n_y, n_z, lanes = dims
    tokens = ROWS * n_seq
    gs_scale = 1.0 / math.sqrt(tokens)
    gl_scale = 1.0 / math.sqrt(tokens * (lanes * n_ch // GROUPS))
    tiles = lanes // 128
    chunks = lanes // 256
    halves = tiles // 4
    s = lax.axis_index("seq")
    ch = lax.axis_index("ch")
    core = lax.rem(s, 2)
    z = lax.rem(s // 2, n_z)
    y = s // (2 * n_z)

    def at(yy, zz, cc):
        return (yy * n_z + zz) * 2 + cc

    ahead = {"seq": lax.rem(s + 1, n_seq)}
    behind = {"seq": lax.rem(s + n_seq - 1, n_seq)}
    sibling = {"seq": at(y, z, 1 - core)}

    def far_first(n):
        return sorted(range(1, n), key=lambda d: -min(d, n - d))

    ys_peers = [{"seq": at(lax.rem(y + d, n_y), z, core)} for d in far_first(n_y)]
    zs_peers = [{"seq": at(y, lax.rem(z + d, n_z), core)} for d in far_first(n_z)]
    n_own = 2 * n_ch
    own = ch * 2 + core
    xc_peers = []
    for d in far_first(n_own):
        o = lax.rem(own + d, n_own)
        xc_peers.append(({"seq": at(y, z, lax.rem(o, 2)), "ch": o // 2}, o))

    barrier = pltpu.get_barrier_semaphore()
    greet = [ahead, behind] + ys_peers + zs_peers + [p for p, _ in xc_peers]
    for p in greet:
        pl.semaphore_signal(barrier, inc=1, device_id=p, device_id_type=MESH)

    def load(src, dst, i):
        c = pltpu.make_async_copy(src, dst, ld_sem.at[i])
        c.start()
        return c

    def all_of(ref, sem):
        pltpu.make_async_copy(ref, ref, sem).wait()

    c_short = load(short, shortv, 0)
    for l in range(tiles):
        load(feat.at[:, LATE:, l * 128 : (l + 1) * 128], fb.at[l, :, LATE:, :], 1)
    for l in range(tiles):
        load(gout.at[:, l * 128 : (l + 1) * 128], gob.at[l], 2)
    for l in range(tiles):
        load(feat.at[:, :LATE, l * 128 : (l + 1) * 128], fb.at[l, :, :LATE, :], 6)
    c_long = load(long, longv, 3)
    c_fwd = load(fwd, fwdv, 4)
    c_inv = load(inv, invv, 5)

    def remote(src, dst, ssem, rsem, peer):
        pltpu.make_async_remote_copy(
            src_ref=src, dst_ref=dst, send_sem=ssem, recv_sem=rsem, device_id=peer, device_id_type=MESH
        ).start()

    c_short.wait()
    for i in range(3):
        taps = shortv[i].astype(F32)
        for l in range(tiles):
            coef[l, i, 0:SHORT, :] = taps[:, l * 128 : (l + 1) * 128]

    def tap(l, i):
        return [coef[l, i, j : j + 1, :] for j in range(SHORT)]

    def fir(ref, l, i, c, first):
        total = c[0] * ref[l, i, first : first + 16, :]
        for j in range(1, SHORT):
            total = total + c[j] * ref[l, i, first - j : first - j + 16, :]
        return total.astype(BF)

    def widen(l, i, lo, hi):
        for r in range(lo, hi, 16):
            xf[l, i, 8 + r : 24 + r, :] = fb[l, i, r : r + 16, :].astype(F32)

    def tile(l):
        return pl.ds(pl.multiple_of(l * 128, 128), 128)

    def lane(l):
        if isinstance(l, int):
            return slice((l % 2) * 128, (l % 2) * 128 + 128)
        return pl.ds(pl.multiple_of(lax.rem(l, 2) * 128, 128), 128)

    def product_rows(l, lo, hi, near=False):
        ck, cv = tap(l, 1), tap(l, 2)
        for r in range(lo, hi, 16):
            k = fir(xf, l, 1, ck, 8 + r)
            v = fir(xf, l, 2, cv, 8 + r)
            kb[l, r : r + 16, :] = k
            vb[l, r : r + 16, :] = v
            p = (k.astype(F32) * v.astype(F32)).astype(BF)
            if near:
                ends[l // 2, 0:16, lane(l)] = p
                ends[l // 2, 16:32, lane(l)] = p
            else:
                prod[l // 2, r : r + 16, lane(l)] = p

    def grad_rows(l, lo, hi, near=False):
        cq = tap(l, 0)
        for r in range(lo, hi, 16):
            q = fir(xf, l, 0, cq, 8 + r)
            g = (q.astype(F32) * gob[l, r : r + 16, :].astype(F32)).astype(BF)
            if near:
                c = (l % 2) * 128 + 256
                ends[l // 2, 0:16, c : c + 128] = g
                ends[l // 2, 16:32, c : c + 128] = g
            else:
                gfil[l // 2, r : r + 16, lane(l)] = g

    def lasts():
        for l in range(tiles):
            for i in range(3):
                widen(l, i, ROWS - 16, ROWS)

    def tail(l, _):
        widen(l, 1, LATE, ROWS - 16)
        widen(l, 2, LATE, ROWS - 16)
        product_rows(l, 128, ROWS)
        return 0

    def tails(q):
        lax.fori_loop(2 * q, 2 * q + 2, tail, 0)

    raw_s = x_s = y_s = g_s = halo_s.at[0]
    pack_s = halo_s.at[1]
    raw_r, pack_r = halo_r.at[0], halo_r.at[1]

    def six(l, i):
        return slice((3 * l + i) * EDGE, (3 * l + i + 1) * EDGE)

    def packs():
        for l in range(tiles):
            for i in range(3):
                packf[six(l, i), :] = xf[l, i, 8 + ROWS - EDGE : 8 + ROWS, :]
        packb[0] = packf[...].astype(BF)

    def send_first():
        pl.semaphore_wait(barrier, len(greet))
        remote(packb.at[0], packb.at[1], pack_s, pack_r, ahead)
        remote(feat.at[0, 0:16, :], raw.at[0], raw_s, raw_r, behind)
        remote(gout.at[0:16, :], raw.at[1], raw_s, raw_r, behind)

    def send_tail(q):
        remote(prod.at[q, ROWS - TAPS :, :], xhalo.at[q], x_s, x_r.at[q], ahead)

    def head(l, _):
        widen(l, 0, 0, 128)
        grad_rows(l, 16, 128)
        return 0

    def heads(q):
        lax.fori_loop(2 * q, 2 * q + 2, head, 0)

    def send_head(q):
        remote(gfil.at[q, 16:TAPS, :], yhalo.at[q, 16:TAPS, :], y_s, y_r.at[q], behind)

    def rest(l):
        widen(l, 0, 128, ROWS - 16)
        grad_rows(l, 128, ROWS)
        widen(l, 1, 0, LATE)
        widen(l, 2, 0, LATE)
        product_rows(l, 16, 128)

    nt = (((1,), (1,)), ((), ()))

    def spectrum():
        hs[...] = lax.dot_general(fwdv[:, 0:TAPS], longv[...], nt, preferred_element_type=F32) + lax.dot_general(
        fwdv[:, ROWS : ROWS + TAPS], longv[...], nt, preferred_element_type=F32
    )

    not_first = jnp.where(s > 0, 1.0, 0.0).astype(F32)
    not_last = jnp.where(s < n_seq - 1, 1.0, 0.0).astype(F32)
    def unpack():
        packf[...] = packb[1].astype(F32) * not_first

    def edges(l):
        cols = slice(l * 128, (l + 1) * 128)
        for i in range(3):
            xf[l, i, 8 - EDGE : 8, :] = packf[six(l, i), :]
        qn[l, 0, 0:8, :] = xf[l, 0, ROWS : ROWS + 8, :]
        qn[l, 0, 8:24, :] = raw[0, :, cols].astype(F32)
        product_rows(l, 0, 16, near=True)
        grad_rows(l, 0, 16, near=True)
        qq = fir(qn, l, 0, tap(l, 0), 8)
        yhalo[l // 2, 0:16, (l % 2) * 128 : (l % 2) * 128 + 128] = (
            qq.astype(F32) * raw[1, :, cols].astype(F32)
        ).astype(BF)

    def dot(a, b):
        return jnp.dot(a, b, preferred_element_type=F32)

    def local(q):
        p = prod[q]
        xs[q] = dot(fwdv[:, 0:ROWS], p) + dot(fwdv[:, ROWS : 2 * ROWS], p)
        g = gfil[q]
        ys[q] = dot(fwdv[:, 0:ROWS], g) + dot(fwdv[:, ROWS : 2 * ROWS], g)


    def far(h):
        return dot(fwdv[:, 2 * ROWS : 2 * ROWS + TAPS], h) + dot(fwdv[:, 2 * ROWS + TAPS : 2 * N], h)

    def wait_x(q):
        all_of(xhalo.at[q], x_r.at[q])

    def wait_y(q):
        all_of(yhalo.at[q, 16:TAPS, :], y_r.at[q])

    def add_x(q):
        wait_x(q)
        xs[q] = xs[q] + not_first * far(xhalo[q])

    def add_y(q):
        wait_y(q)
        ys[q] = ys[q] - not_last * far(yhalo[q])

    def both(halo, sign, near):
        h = (halo.astype(F32) * sign).astype(BF)
        return dot(fwdv[:, 2 * ROWS :], jnp.concatenate([h, h, near], axis=0))

    def add_ends(q):
        if q < chunks // 2:
            wait_x(q)
            xs[q] = xs[q] + both(xhalo[q], not_first, ends[q, :, 0:256])
            ys[q] = ys[q] + dot(fwdv[:, 2 * N :], ends[q, :, 256:512])
        else:
            wait_y(q)
            ys[q] = ys[q] + both(yhalo[q], -not_last, ends[q, :, 256:512])
            xs[q] = xs[q] + dot(fwdv[:, 2 * N :], ends[q, :, 0:256])

    def corr(q, first):
        def block(b, _):
            re = pl.ds(pl.multiple_of(b * 16, 16), 16)
            im = pl.ds(pl.multiple_of(b * 16 + HALF, 16), 16)
            xr, xi, yr, yi = xs[q, re, :], xs[q, im, :], ys[q, re, :], ys[q, im, :]
            rr = xr * yr + xi * yi
            ri = xr * yi - xi * yr
            if not first:
                rr = rr + rs[re, :]
                ri = ri + rs[im, :]
            rs[re, :] = rr
            rs[im, :] = ri
            return 0

        lax.fori_loop(0, HALF // 16, block, 0, unroll=True)

    def hilo(value):
        high = value.astype(BF)
        return high, (value - high.astype(F32)).astype(BF)

    own_rows = TAPS // n_own

    def piece(o):
        return pl.ds(pl.multiple_of(o * own_rows, own_rows), own_rows)

    def lags():
        rh, rl = hilo(rs[...])
        glp[...] = (
            dot(invv[0:TAPS, 0:N], rh) + dot(invv[0:TAPS, N:], rh) + dot(invv[0:TAPS, 0:N], rl)
        ).astype(BF)

    rings = ((ys_peers, zs_peers), (zs_peers, ys_peers))
    places = ((y, z), (z, y))

    def spread(rsems, ssem, refs, values, step):
        for k in range(2):
            refs[k][places[k][step]] = values[k]
        for i in range(max(n_y, n_z) - 1):
            for k in range(2):
                if i < len(rings[k][step]):
                    slot = refs[k].at[places[k][step]]
                    remote(slot, slot, ssem, rsems[k], rings[k][step][i])

    def gathered(ref, sem, count):
        all_of(ref.at[0 : count - 1], sem)
        total = ref[0].astype(F32)
        for d in range(1, count):
            total = total + ref[d].astype(F32)
        return total

    counts = ((n_y, n_z), (n_z, n_y))

    def gl_zero():
        glrecv[own] = glp[piece(own), :]
        for p, o in xc_peers:
            remote(glp.at[piece(o), :], glrecv.at[own], gl_s, gl_r.at[0], p)

    def gl_one():
        total = gathered(glrecv, gl_r.at[0], n_own).astype(BF)
        sems = [gl_r.at[1 + k] for k in range(2)]
        spread(sems, gl_s, [glex.at[k] for k in range(2)], [total[:, :128], total[:, 128:]], 0)

    def gl_two():
        parts = [gathered(glex.at[k], gl_r.at[1 + k], counts[k][0]).astype(BF) for k in range(2)]
        sems = [gl_r.at[3 + k] for k in range(2)]
        spread(sems, gl_s, [glex2.at[k] for k in range(2)], parts, 1)

    def gl_three():
        for k in range(2):
            total = gathered(glex2.at[k], gl_r.at[3 + k], counts[k][1]) * gl_scale
            glfin[piece(own), k * 128 : (k + 1) * 128] = total.astype(BF)
        for p, _ in xc_peers:
            remote(glfin.at[piece(own), :], glfin.at[piece(own), :], gl_s, gl_r.at[5], p)

    def gl_four():
        all_of(glfin.at[0 : TAPS - own_rows], gl_r.at[5])
        gl_out[...] = glfin[...].astype(F32).T

    def gs_zero(h):
        theirs = pl.ds(4 * h + 2 * (1 - core), 2)
        remote(gsp.at[theirs], gscore.at[h], gs_s.at[h], gs_r.at[h, 0], sibling)

    def part_rows(h, k):
        cut = 32 if h % 2 == 0 else 16
        return slice(0, cut) if k == 0 else slice(cut, 48)

    def gs_one(h):
        all_of(gscore.at[h], gs_r.at[h, 0])
        total = gsp[pl.ds(4 * h + 2 * core, 2)] + gscore[h]
        total = total.reshape(48, 128)
        rows = [part_rows(h, k) for k in range(2)]
        sems = [gs_r.at[h, 1 + k] for k in range(2)]
        spread(sems, gs_s.at[h], [gsex.at[h, :, r, :] for r in rows], [total[r].astype(BF) for r in rows], 0)

    def gs_two(h):
        rows = [part_rows(h, k) for k in range(2)]
        parts = [
            gathered(gsex.at[h, :, rows[k], :], gs_r.at[h, 1 + k], counts[k][0]).astype(BF) for k in range(2)
        ]
        sems = [gs_r.at[h, 3 + k] for k in range(2)]
        spread(sems, gs_s.at[h], [gsex2.at[h, :, r, :] for r in rows], parts, 1)

    def gs_three(h):
        parts = []
        for k in range(2):
            ref = gsex2.at[h, :, part_rows(h, k), :]
            parts.append(gathered(ref, gs_r.at[h, 3 + k], counts[k][1]))
        total = jnp.concatenate(parts, axis=0) * gs_scale
        here = pl.ds(4 * h + 2 * core, 2)
        gsfin[here] = total.reshape(2, 24, 128)
        remote(gsfin.at[here], gsfin.at[here], gs_s.at[h], gs_r.at[h, 5], sibling)

    def gs_four(h):
        all_of(gscore.at[h], gs_r.at[h, 5])
        for l in range(4 * h, 4 * h + 4):
            for i in range(3):
                gs_out[i, :, l * 128 : (l + 1) * 128] = gsfin[l, 8 * i : 8 * i + SHORT, :]

    def spectra(q):
        def block(b, _):
            re = pl.ds(pl.multiple_of(b * 16, 16), 16)
            im = pl.ds(pl.multiple_of(b * 16 + HALF, 16), 16)
            hr, hi = hs[re, :], hs[im, :]
            xr, xi = xs[q, re, :], xs[q, im, :]
            yr, yi = ys[q, re, :], ys[q, im, :]
            parts = (
                (re, 0, xr * hr - xi * hi),
                (im, 0, xr * hi + xi * hr),
                (re, 256, yr * hr + yi * hi),
                (im, 256, yi * hr - yr * hi),
            )
            for rows, c, value in parts:
                spec[rows, c : c + 256] = value.astype(BF)
            return 0

        lax.fori_loop(0, HALF // 16, block, 0, unroll=3)

    def inverse():
        filt[...] = dot(invv[:, 0:N], spec[...])

    def featured_grad(l, h):
        for r in range(0, ROWS, 16):
            rows = slice(r, r + 16)
            fa = filt[rows, h * 128 : h * 128 + 128]
            fg = filt[rows, 256 + h * 128 : 256 + h * 128 + 128]
            g0 = (gob[l, rows, :].astype(F32) * fa).astype(BF)
            g1 = (fg * vb[l, rows, :].astype(F32)).astype(BF)
            g2 = (fg * kb[l, rows, :].astype(F32)).astype(BF)
            for i, g in enumerate((g0, g1, g2)):
                gf[l, i, rows, :] = g.astype(F32)

    def short_grad(l):
        for i in range(3):
            acc = [jnp.zeros((8, 128), F32) for _ in range(SHORT)]
            for r in range(0, ROWS, 8):
                g = gf[l, i, r : r + 8, :]
                for j in range(SHORT):
                    acc[j] = acc[j] + g * xf[l, i, 8 + r - j : 16 + r - j, :]
            rows = [jnp.sum(a, axis=0, keepdims=True) for a in acc]
            rows.append(jnp.zeros((1, 128), F32))
            gsp[l, 8 * i : 8 * i + 8, :] = jnp.concatenate(rows, axis=0)

    def fgrads(q):
        for h in range(2):
            featured_grad(2 * q + h, h)

    def send_grad(q):
        for h in range(2):
            for i in range(3):
                gpack[six(h, i), :] = gf[2 * q + h, i, 0:EDGE, :]
        gedge[0, q] = gpack[...].astype(BF)
        remote(gedge.at[0, q], gedge.at[1, q], g_s, g_r.at[q], behind)

    def sgrads(q):
        def sg(l, _):
            short_grad(l)
            return 0

        lax.fori_loop(2 * q, 2 * q + 2, sg, 0)

    def wait_grad(q):
        all_of(gedge.at[1, q], g_r.at[q])

    def conv(q):
        wait_grad(q)
        gpack[...] = gedge[1, q].astype(F32) * not_last
        for h in range(2):
            for i in range(3):
                gf[2 * q + h, i, ROWS : ROWS + EDGE, :] = gpack[six(h, i), :]

        def one(l, _):
            for i in range(3):
                c = tap(l, i)
                for r in range(0, ROWS, 16):
                    total = c[0] * gf[l, i, r : r + 16, :]
                    for j in range(1, SHORT):
                        total = total + c[j] * gf[l, i, r + j : r + j + 16, :]
                    out[i, r : r + 16, tile(l)] = total.astype(BF)
            return 0

        lax.fori_loop(2 * q, 2 * q + 2, one, 0)

    for q in range(chunks):
        prod[q, 0:16, :] = jnp.zeros((16, 256), BF)
        gfil[q, 0:16, :] = jnp.zeros((16, 256), BF)
        ends[q, 32:, :] = jnp.zeros((96, 512), BF)
    gpack[6 * EDGE :, :] = jnp.zeros((48 - 6 * EDGE, 128), F32)
    all_of(fb.at[:, :, LATE:, :], ld_sem.at[1])
    lasts()
    packs()
    first, second = list(range(chunks // 2)), list(range(chunks // 2, chunks))
    for q in first:
        tails(q)
    send_first()
    for q in first:
        send_tail(q)
    all_of(gob, ld_sem.at[2])
    all_of(fb.at[:, :, :LATE, :], ld_sem.at[6])
    for q in second:
        heads(q)
        send_head(q)
    for q in second:
        tails(q)
        send_tail(q)
    for q in first:
        heads(q)
        send_head(q)
    c_fwd.wait()
    for q in range(chunks):
        rest(2 * q)
        rest(2 * q + 1)
        local(q)
    all_of(packb.at[1], pack_r)
    all_of(raw, raw_r)
    unpack()
    for l in range(tiles):
        edges(l)
    for q in range(chunks // 2):
        add_ends(q)
        corr(q, q == 0)
        add_ends(q + chunks // 2)
        corr(q + chunks // 2, False)
    c_inv.wait()
    lags()
    gl_zero()
    c_long.wait()
    spectrum()

    def chunk(h, c):
        q = 2 * h + c
        if h < halves // 2:
            add_y(q)
        else:
            add_x(q)
        spectra(q)
        inverse()
        fgrads(q)
        send_grad(q)
        sgrads(q)

    chunk(0, 1 - core)
    gs_zero(0)
    chunk(0, core)
    gs_one(0)
    chunk(1, 1 - core)
    gs_zero(1)
    gl_one()
    chunk(1, core)
    gs_one(1)
    conv(0)
    conv(1)
    conv(2)
    conv(3)
    gs_two(0)
    gl_two()
    gs_two(1)
    gl_three()
    gs_three(0)
    gs_three(1)
    gs_four(0)
    gl_four()
    gs_four(1)

    def left(sem, *refs):
        size = sum(math.prod(r.shape) * jnp.dtype(r.dtype).itemsize for r in refs)
        lines = size // 1024
        view = xs.at[0, 0:lines, :] if lines <= N else xs.at[0:2, 0 : lines // 2, :]
        assert math.prod(view.shape) * 4 == size
        all_of(view, sem)

    all_of(packb.at[0], pack_s)
    left(halo_s.at[0], raw, xhalo, yhalo.at[:, 16:TAPS, :], gedge.at[0])
    sent = [glrecv.at[0 : n_own - 1]] * 2
    for k in range(2):
        sent += [glex.at[k, 0 : counts[k][0] - 1], glex2.at[k, 0 : counts[k][1] - 1]]
    left(gl_s, *sent)
    for h in range(halves):
        sent = [gscore.at[h]] * 2
        for k in range(2):
            rows = part_rows(h, k)
            sent += [gsex.at[h, 0 : counts[k][0] - 1, rows, :], gsex2.at[h, 0 : counts[k][1] - 1, rows, :]]
        left(gs_s.at[h], *sent)


def emit(*refs):
    sem = refs[-1]
    copies = [pltpu.make_async_copy(refs[i], refs[3 + i], sem.at[i]) for i in range(3)]
    for c in copies:
        c.start()
    for c in copies:
        c.wait()


def solution(mesh):
    n_seq, n_ch = mesh.shape["seq"], mesh.shape["ch"]
    n_z = math.isqrt(n_seq // 2)
    n_y = n_seq // (2 * n_z)
    forward, inverse = transforms()

    def body(features, short_filter, long_filter, grad_out):
        lanes = features.shape[2]
        tiles, chunks, halves = lanes // 128, lanes // 256, lanes // 512
        n_own = 2 * n_ch
        own_rows = TAPS // n_own
        most = max(n_y, n_z)
        any_spec = pl.BlockSpec(memory_space=pltpu.HBM)
        vmem = pl.BlockSpec(memory_space=pltpu.VMEM)
        V = pltpu.VMEM
        D = pltpu.SemaphoreType.DMA
        results = pl.pallas_call(
            functools.partial(kernel, (n_seq, n_ch, n_y, n_z, lanes)),
            out_shape=(
                V((3, ROWS, lanes), BF),
                V((3, SHORT, lanes), F32),
                V((GROUPS, TAPS), F32),
            ),
            in_specs=[any_spec] * 6,
            out_specs=(vmem, vmem, vmem),
            scratch_shapes=[
                V((tiles, 3, ROWS, 128), BF),
                V((tiles, ROWS, 128), BF),
                V((N, 2 * N + 128), BF),
                V((ROWS, 2 * N), BF),
                V((3, SHORT, lanes), BF),
                V((GROUPS, TAPS), BF),
                V((tiles, 3, 8, 128), F32),
                V((tiles, 3, ROWS + 8, 128), F32),
                V((tiles, ROWS, 128), BF),
                V((tiles, ROWS, 128), BF),
                V((chunks, ROWS, 256), BF),
                V((chunks, ROWS, 256), BF),
                V((chunks, 128, 512), BF),
                V((chunks, TAPS, 256), BF),
                V((chunks, TAPS, 256), BF),
                V((2, 16, lanes), BF),
                V((tiles * 3 * EDGE, 128), F32),
                V((2, tiles * 3 * EDGE, 128), BF),
                V((tiles, 1, 24, 128), F32),
                V((N, 256), F32),
                V((chunks, N, 256), F32),
                V((chunks, N, 256), F32),
                V((N, 256), F32),
                V((N, 512), BF),
                V((ROWS, 512), F32),
                V((tiles, 3, ROWS + 8, 128), F32),
                V((48, 128), F32),
                V((2, chunks, 48, 128), BF),
                V((TAPS, 256), BF),
                V((n_own, own_rows, 256), BF),
                V((2, most, own_rows, 128), BF),
                V((2, most, own_rows, 128), BF),
                V((TAPS, 256), BF),
                V((tiles, 24, 128), F32),
                V((halves, 2, 24, 128), F32),
                V((halves, most, 48, 128), BF),
                V((halves, most, 48, 128), BF),
                V((tiles, 24, 128), F32),
                D((7,)),
                D((2,)),
                D((2,)),
                D((chunks,)),
                D((chunks,)),
                D((chunks,)),
                D,
                D((6,)),
                D((halves,)),
                D((halves, 6)),
            ],
            compiler_params=pltpu.CompilerParams(
                collective_id=0, has_side_effects=True, vmem_limit_bytes=40 * 2**20
            ),
            name="hyena_backward",
        )(
            *(
                pltpu.with_memory_space_constraint(a, pltpu.HBM)
                for a in (features, short_filter, long_filter, grad_out, jnp.asarray(forward), jnp.asarray(inverse))
            )
        )
        grad_features, grad_short, grad_long = pl.pallas_call(
            emit,
            out_shape=tuple(jax.ShapeDtypeStruct(r.shape, r.dtype) for r in results),
            in_specs=[vmem] * 3,
            out_specs=(pl.BlockSpec(memory_space=pl.ANY),) * 3,
            scratch_shapes=[D((3,))],
            name="emit",
        )(*(pltpu.with_memory_space_constraint(r, pltpu.VMEM) for r in results))
        return grad_features, grad_short, grad_long

    return jax.shard_map(
        body,
        mesh=mesh,
        in_specs=(P(None, "seq", "ch"), P(None, None, "ch"), P(), P("seq", "ch")),
        out_specs=(P(None, "seq", "ch"), P(None, None, "ch"), P()),
        check_vma=False,
    )
```
